32 devices in a mesh: dp: 16 (over z, y, x), tensor: 2 (over core).
Axes of the slice: x: 2, y: 2, z: 4, core: 2. Of those that a mesh axis runs over, the one named last changes fastest.
Arguments:
- hidden: bfloat16 [48, 256, 14336], P('dp', None, 'tensor'), may hold values from -6 to 6
- out_grad: bfloat16 [48, 256, 4096], P('dp', None, 'tensor'), may hold values from -0.29882812 to 0.29882812
- proj_in: bfloat16 [64, 14336], P(None, 'tensor'), may hold values from -0.046875 to 0.046875
- proj_out: bfloat16 [64, 4096], P(None, 'tensor'), may hold values from -0.09375 to 0.09375
- left_inv: float32 [64, 64], replicated, may hold values from -0.15 to 3, as said below
- right_inv: float32 [64, 64], replicated, may hold values from -0.15 to 3, as said below
- lengths: int32 [48], P('dp'), may hold values from 64 to 256
- language: int32 [48], P('dp'), may hold values from 0 to 99
- owner: int32 [100], replicated, may hold values from 0 to 15, as said below
Outputs:
- seq_grads: float32 [48, 4096], P('dp', 'tensor')
- owned_means: float32 [112, 4096], P('dp', 'tensor')
The draws below stay inside these ranges and needn't reach their ends.
Inputs may be any that keep to these rules, and one draw needn't show every extreme that they name: `left_inv`: symmetric; diagonal entries 1 or more, off-diagonal entries of magnitude 0.15 or less. `right_inv`: symmetric; diagonal entries 1 or more, off-diagonal entries of magnitude 0.15 or less. Every owner holds 6 or 7 languages, and some owner holds 7.
All inputs are finite; a program needn't handle non-finite values.
Results may differ from the reference program's by a relative error of at most 0.0003.
Values sent between devices are 32-bit elements; how exact they have to be, the bound alone decides.
A program may use at most 64 MiB of HBM per device.

```python
import math
import jax
import jax.numpy as jnp
import numpy as np
from jax import lax

D = 4096
FF = 14336
R = 64
LANGS = 100
SEQ_LEN = 256
SEQS = 48
OWNERS = 16
SLOTS = 7
OWNED = 112


def inverse_factor(key):
    off_key, diag_key = jax.random.split(key)
    spread = 0.1
    lower_end = 1.0
    upper_end = 2.0
    off_part = jax.random.uniform(off_key, (R, R), jnp.float32, -spread, spread)
    off_part = 0.5 * (off_part + off_part.T)
    diagonal = jax.random.uniform(diag_key, (R,), jnp.float32, lower_end, upper_end)
    identity = jnp.eye(R, dtype=jnp.float32)
    return off_part * (1.0 - identity) + identity * diagonal[None, :]


def draw_left_inv(key, part):
    return inverse_factor(jax.random.fold_in(key, 11))


def draw_right_inv(key, part):
    return inverse_factor(jax.random.fold_in(key, 23))


def draw_owner(key, part):
    order = jax.random.permutation(jax.random.fold_in(key, 37), LANGS)
    return (order % OWNERS).astype(jnp.int32)


def place_ends(drawn, rng, smallest, largest):
    longest = drawn.shape.index(max(drawn.shape))
    spots = []
    for shift in (0, 1):
        where = [jax.random.randint(jax.random.fold_in(rng, axis), (), 0, length) for axis, length in enumerate(drawn.shape)]
        where[longest] = (where[longest] + shift) % drawn.shape[longest]
        spots.append(tuple(where))
    return drawn.at[spots[0]].set(smallest).at[spots[1]].set(largest)


def shard_levels(rng, dims, cuts, least, largest):
    level, own = 1.0, jax.random.fold_in(rng, 6)
    for position, parts in cuts:
        heights = jnp.exp(jax.random.uniform(jax.random.fold_in(own, position), (parts,), jnp.float32, least / len(cuts), largest / len(cuts)))
        level = level * jnp.repeat(heights, dims[position] // parts).reshape([-1 if axis == position else 1 for axis in range(len(dims))])
    return level


def cumulative_ranks(count, lean):
    weights = [(1 << 20) // math.isqrt(standing ** lean) + 1 for standing in range(1, count + 1)]
    deviation = 1 + sum(weights) // (1 << 30)
    return np.cumsum(np.array([max(1, weight // deviation) for weight in weights]))


def skewed_ids(key, extent, number_of, lean):
    grid = cumulative_ranks(number_of, lean)
    ticket = jax.random.randint(jax.random.fold_in(key, 1), extent, 0, int(grid[number_of - 1]))
    standing = jnp.searchsorted(jnp.asarray(grid, jnp.int32), ticket, side="right")
    return jax.random.permutation(jax.random.fold_in(key, 2), number_of)[standing].astype(jnp.int32)


def scatter_about(own_key, extent, scale, limit, pieces=(), kind=jnp.bfloat16):
    values = scale * jax.random.normal(own_key, extent, jnp.float32)
    if pieces:
        values = values * shard_levels(own_key, extent, pieces, -0.22, 0.18)
    return jnp.clip(values, -limit, limit).astype(kind)


def setup_inputs(seed: int = 0) -> dict:
    streams_of = jax.random.split(jax.random.key(seed), 10)
    return {
        "hidden": scatter_about(streams_of[0], (SEQS, SEQ_LEN, FF), 1.0, 6.0, ((0, 16), (2, 2))),
        "out_grad": scatter_about(streams_of[1], (SEQS, SEQ_LEN, D), 0.05, 0.29882812, ((0, 16), (2, 2))),
        "proj_in": scatter_about(streams_of[2], (R, FF), FF ** -0.5, 0.046875, ((1, 2),)),
        "proj_out": scatter_about(streams_of[3], (R, D), D ** -0.5, 0.09375, ((1, 2),)),
        "left_inv": draw_left_inv(jax.random.fold_in(streams_of[9], 71), 0),
        "right_inv": draw_right_inv(jax.random.fold_in(streams_of[9], 71), 0),
        "lengths": place_ends(jax.random.randint(streams_of[6], (SEQS,), SEQ_LEN // 4, SEQ_LEN + 1), jax.random.fold_in(streams_of[6], 1), SEQ_LEN // 4, SEQ_LEN).astype(jnp.int32),
        "language": place_ends(skewed_ids(streams_of[7], (SEQS,), LANGS, 2), jax.random.fold_in(streams_of[7], 3), 0, LANGS - 1).astype(jnp.int32),
        "owner": draw_owner(jax.random.fold_in(streams_of[9], 71), 0),
    }


def project(values, projection):
    flattened = values.reshape(-1, values.shape[-1])
    return lax.dot_general(flattened, projection, (((1,), (1,)), ((), ())), preferred_element_type=jnp.float32)


def reference(hidden, out_grad, proj_in, proj_out, left_inv, right_inv, lengths, language, owner):
    highest = lax.Precision.HIGHEST
    left_full = project(hidden, proj_in).reshape(SEQS, SEQ_LEN, R)
    right_full = project(out_grad, proj_out).reshape(SEQS, SEQ_LEN, R)
    token_mask = (jnp.arange(SEQ_LEN, dtype=jnp.int32)[None, :] < lengths[:, None]).astype(jnp.float32)
    right_full = right_full * token_mask[:, :, None]
    seq_grads = jnp.einsum("sti,stj->sij", left_full, right_full, precision=highest)
    left_done = jnp.einsum("ik,skj->sij", left_inv, seq_grads, precision=highest)
    preconditioned = jnp.einsum("sik,kj->sij", left_done, right_inv, precision=highest)
    lang_index = jnp.arange(LANGS, dtype=jnp.int32)
    lang_hot = (language[:, None] == lang_index[None, :]).astype(jnp.float32)
    lang_count = jnp.sum(lang_hot, axis=0)
    lang_total_sum = jnp.dot(lang_hot.T, preconditioned.reshape(SEQS, R * R), precision=highest)
    lang_mean = lang_total_sum / jnp.maximum(lang_count, 1.0)[:, None]
    same_owner = (owner[:, None] == owner[None, :]) & (lang_index[None, :] < lang_index[:, None])
    lang_slot = jnp.sum(same_owner.astype(jnp.int32), axis=1)
    lang_place = owner * SLOTS + lang_slot
    place_hot = (lang_place[:, None] == jnp.arange(OWNED, dtype=jnp.int32)[None, :]).astype(jnp.float32)
    owned_means = jnp.dot(place_hot.T, lang_mean, precision=highest)
    return seq_grads.reshape(SEQS, R * R), owned_means
```

```python
import functools
import math

import jax
import jax.numpy as jnp
from jax import lax
from jax.experimental import pallas as pl
from jax.experimental.pallas import tpu as pltpu
from jax.sharding import PartitionSpec as P

LANES = 128
HIGHEST = lax.Precision.HIGHEST


def pieces_of(width):
    for count in (4, 2):
        if width % (count * 256) == 0:
            return count
    return 1


def kernel(
    sizes,
    lengths,
    language,
    owner_list,
    owner_row,
    left_inv,
    right_inv,
    hidden,
    out_grad,
    proj_in,
    proj_out,
    grads_out,
    means_out,
    hid,
    og,
    w_in,
    w_out,
    part,
    peer_part,
    g_scr,
    gathered,
    places,
    hid_sem,
    og_sem,
    w_sem,
    t_send,
    t_recv,
    z_send,
    z_recv,
    p_send,
    p_recv,
    m_send,
    m_recv,
):
    t_size, outer, inner, slots = sizes
    seqs, tokens, hid_width = hid.shape
    rank = w_in.shape[0]
    half = rank // t_size
    rows = half // 2
    dp = lax.axis_index("dp")
    t_me = lax.axis_index("tensor")
    my_out = dp // inner
    my_in = dp % inner
    hid_pieces = pieces_of(hid_width)
    piece = hid_width // hid_pieces

    w_in_copy = pltpu.make_async_copy(proj_in, w_in, w_sem.at[0])
    w_out_copy = pltpu.make_async_copy(proj_out, w_out, w_sem.at[1])
    w_out_copy.start()
    og_copies = []
    hid_copies = []
    for s in range(seqs):
        og_copies.append(pltpu.make_async_copy(out_grad.at[s], og.at[s], og_sem.at[s]))
        og_copies[s].start()
        if s == 0:
            w_in_copy.start()
        for c in range(hid_pieces):
            cols = pl.ds(c * piece, piece)
            hid_copies.append(
                pltpu.make_async_copy(
                    hidden.at[s, :, cols], hid.at[s, :, cols], hid_sem.at[s, c]
                )
            )
            hid_copies[-1].start()

    def t_peer(k):
        return (dp, (t_me + k) % t_size)

    def z_peer(k):
        return (((my_out + k) % outer) * inner + my_in, t_me)

    def p_peer(k):
        return (my_out * inner + (my_in + k) % inner, t_me)

    peers = [(t_peer, t_size), (z_peer, outer), (p_peer, inner)]
    barrier = pltpu.get_barrier_semaphore()
    for peer_of, count in peers:
        for k in range(1, count):
            pl.semaphore_signal(
                barrier, inc=1, device_id=peer_of(k), device_id_type=pl.DeviceIdType.MESH
            )

    own_row = owner_row[...]
    lang_lane = lax.broadcasted_iota(jnp.int32, own_row.shape, 1)
    sub = lax.broadcasted_iota(jnp.int32, places.shape[2:], 0)
    place_block = jnp.full(places.shape[2:], -1, jnp.int32)
    for s in range(seqs):
        lang = language[s]
        own = owner_list[lang]
        earlier = (own_row == own) & (lang_lane < lang)
        slot = jnp.sum(earlier.astype(jnp.int32), axis=1, keepdims=True)
        place_block = jnp.where(sub == s, own * slots + slot, place_block)
    places[my_in, my_out] = place_block

    def send(src, dst, send_sem, recv_sem, peer):
        pltpu.make_async_remote_copy(
            src_ref=src,
            dst_ref=dst,
            send_sem=send_sem,
            recv_sem=recv_sem,
            device_id=peer,
            device_id_type=pl.DeviceIdType.MESH,
        ).start()

    def take(block, sem):
        pltpu.make_async_copy(block, block, sem).wait()

    def project(s):
        og_copies[s].wait()
        dims = (((1,), (1,)), ((), ()))
        right = lax.dot_general(og[s], w_out[...], dims, preferred_element_type=jnp.float32)
        left = jnp.zeros((tokens, rank), jnp.float32)
        for c in range(hid_pieces):
            if s == 0 and c == 0:
                w_in_copy.wait()
            hid_copies[s * hid_pieces + c].wait()
            cols = slice(c * piece, (c + 1) * piece)
            left += lax.dot_general(
                hid[s, :, cols], w_in[:, cols], dims, preferred_element_type=jnp.float32
            )
        part[s] = jnp.concatenate([left, right], axis=1)

    def send_part(s):
        for k in range(1, t_size):
            send(part.at[s], peer_part.at[s, k - 1], t_send.at[s], t_recv.at[s], t_peer(k))

    first = t_me * half
    even = pl.ds(first, rows, stride=2)
    odd = pl.ds(first + 1, rows, stride=2)

    def reduce(s):
        if t_size > 1:
            take(peer_part.at[s], t_recv.at[s])
        both = part[s]
        for k in range(1, t_size):
            both += peer_part[s, k - 1]
        token = lax.broadcasted_iota(jnp.int32, both.shape, 0)
        both = jnp.where(token < lengths[s], both, 0.0)
        high = both.astype(jnp.bfloat16)
        low = (both - high.astype(jnp.float32)).astype(jnp.bfloat16)
        split = jnp.concatenate([high, low], axis=1)
        full = lax.dot_general(
            split, split, (((0,), (0,)), ((), ())), preferred_element_type=jnp.float32
        )
        wide = 2 * rank
        full = full[0:rank] + full[wide : wide + rank]
        full = full[:, 0:wide] + full[:, wide : 2 * wide]
        grads = full[:, rank:wide]
        g_scr[s] = grads
        left_rows = jnp.concatenate([left_inv[even, :], left_inv[odd, :]], axis=0)
        done = jnp.dot(left_rows, grads, precision=HIGHEST, preferred_element_type=jnp.float32)
        pre = jnp.dot(
            done, right_inv[...], precision=HIGHEST, preferred_element_type=jnp.float32
        )
        gathered[s, my_in, my_out] = jnp.concatenate([pre[:rows], pre[rows:]], axis=1)
        for k in range(1, outer):
            block = gathered.at[s, my_in, my_out]
            send(block, block, z_send.at[s], z_recv.at[s], z_peer(k))
        pair = jnp.concatenate([g_scr[s, even, :], g_scr[s, odd, :]], axis=1)
        for r in range(rows):
            grads_out[s : s + 1, r * LANES : (r + 1) * LANES] = pair[r : r + 1]

    def forward(s):
        if s == 0:
            if outer > 1:
                take(places.at[0, pl.ds(0, outer - 1)], m_recv.at[0])
            for k in range(1, inner):
                block = places.at[my_in]
                send(block, block, m_send.at[1], m_recv.at[1], p_peer(k))
        if outer > 1:
            take(gathered.at[s, 0, pl.ds(0, outer - 1)], z_recv.at[s])
        for k in range(1, inner):
            block = gathered.at[s, my_in]
            send(block, block, p_send.at[s], p_recv.at[s], p_peer(k))

    def accumulate(s, held):
        if s == 0 and inner > 1:
            take(places.at[pl.ds(0, inner - 1)], m_recv.at[1])
        if inner > 1:
            take(gathered.at[s, pl.ds(0, inner - 1)], p_recv.at[s])

        def step(i, held):
            sums, counts = held
            sums, counts = list(sums), list(counts)
            for o in range(outer):
                place = places[i, o, s : s + 1, :]
                row = gathered[s, i, o]
                for j in range(slots):
                    hit = (place == dp * slots + j).astype(jnp.float32)
                    sums[j] = sums[j] + hit * row
                    counts[j] = counts[j] + hit
            return tuple(sums), tuple(counts)

        return lax.fori_loop(0, inner, step, held)

    w_out_copy.wait()
    for s in range(seqs):
        project(s)
        if s == 0:
            pl.semaphore_wait(barrier, sum(count - 1 for _, count in peers))
            for k in range(1, outer):
                block = places.at[my_in, my_out]
                send(block, block, m_send.at[0], m_recv.at[0], z_peer(k))
        send_part(s)
        if s >= 2:
            forward(s - 2)
        if s >= 1:
            reduce(s - 1)
    if seqs >= 2:
        forward(seqs - 2)
    reduce(seqs - 1)
    held = (
        tuple(jnp.zeros((rows, LANES), jnp.float32) for _ in range(slots)),
        tuple(jnp.zeros((1, LANES), jnp.float32) for _ in range(slots)),
    )
    for s in range(seqs - 2):
        held = accumulate(s, held)
    forward(seqs - 1)
    for s in range(max(seqs - 2, 0), seqs):
        held = accumulate(s, held)
    sums, counts = held
    for j in range(slots):
        mean = sums[j] / jnp.maximum(counts[j], 1.0)
        for r in range(rows):
            means_out[j : j + 1, r * LANES : (r + 1) * LANES] = mean[r : r + 1]

    for s in range(seqs):
        if t_size > 1:
            take(peer_part.at[s], t_send.at[s])
        if outer > 1:
            take(gathered.at[s, 0, pl.ds(0, outer - 1)], z_send.at[s])
        if inner > 1:
            take(gathered.at[s, pl.ds(0, inner - 1)], p_send.at[s])
    if outer > 1:
        take(places.at[0, pl.ds(0, outer - 1)], m_send.at[0])
    if inner > 1:
        take(places.at[pl.ds(0, inner - 1)], m_send.at[1])


def per_device(hidden, out_grad, proj_in, proj_out, left_inv, right_inv, lengths, language, owner):
    seqs, tokens, hid_width = hidden.shape
    og_width = out_grad.shape[2]
    rank = proj_in.shape[0]
    t_size = lax.axis_size("tensor")
    dp_size = lax.axis_size("dp")
    inner = 2 ** (int(math.log2(dp_size)) // 2)
    while dp_size % inner:
        inner -= 1
    outer = dp_size // inner
    slots = (owner.shape[0] + dp_size - 1) // dp_size
    half = rank // t_size
    rows = half * rank // LANES
    smem = pl.BlockSpec(memory_space=pltpu.SMEM)
    vmem = pl.BlockSpec(memory_space=pltpu.VMEM)
    anywhere = pl.BlockSpec(memory_space=pl.ANY)
    dma = pltpu.SemaphoreType.DMA
    flops = 2 * seqs * tokens * rank * (hid_width + og_width)
    return pl.pallas_call(
        functools.partial(kernel, (t_size, outer, inner, slots)),
        out_shape=(
            jax.ShapeDtypeStruct((seqs, half * rank), jnp.float32),
            jax.ShapeDtypeStruct((slots, half * rank), jnp.float32),
        ),
        in_specs=[smem, smem, smem, vmem, vmem, vmem] + [anywhere] * 4,
        out_specs=(vmem, vmem),
        scratch_shapes=[
            pltpu.VMEM((seqs, tokens, hid_width), jnp.bfloat16),
            pltpu.VMEM((seqs, tokens, og_width), jnp.bfloat16),
            pltpu.VMEM((rank, hid_width), jnp.bfloat16),
            pltpu.VMEM((rank, og_width), jnp.bfloat16),
            pltpu.VMEM((seqs, tokens, 2 * rank), jnp.float32),
            pltpu.VMEM((seqs, max(t_size - 1, 1), tokens, 2 * rank), jnp.float32),
            pltpu.VMEM((seqs, rank, rank), jnp.float32),
            pltpu.VMEM((seqs, inner, outer, rows, LANES), jnp.float32),
            pltpu.VMEM((inner, outer, 8 * ((seqs + 7) // 8), LANES), jnp.int32),
            dma((seqs, pieces_of(hid_width))),
            dma((seqs,)),
            dma((2,)),
            dma((seqs,)),
            dma((seqs,)),
            dma((seqs,)),
            dma((seqs,)),
            dma((seqs,)),
            dma((seqs,)),
            dma((2,)),
            dma((2,)),
        ],
        compiler_params=pltpu.CompilerParams(
            collective_id=0, has_side_effects=True, vmem_limit_bytes=48 * 1024 * 1024
        ),
        cost_estimate=pl.CostEstimate(
            flops=flops,
            bytes_accessed=2 * (seqs * tokens + rank) * (hid_width + og_width),
            transcendentals=0,
        ),
    )(
        lengths,
        language,
        owner,
        owner.reshape(1, -1),
        left_inv,
        right_inv,
        hidden,
        out_grad,
        proj_in,
        proj_out,
    )


def solution(mesh):
    return jax.shard_map(
        per_device,
        mesh=mesh,
        in_specs=(
            P("dp", None, "tensor"),
            P("dp", None, "tensor"),
            P(None, "tensor"),
            P(None, "tensor"),
            P(),
            P(),
            P("dp"),
            P("dp"),
            P(),
        ),
        out_specs=(P("dp", "tensor"), P("dp", "tensor")),
        check_vma=False,
    )
```

```python
import functools
import math

import jax
import jax.numpy as jnp
from jax import lax
from jax.experimental import pallas as pl
from jax.experimental.pallas import tpu as pltpu
from jax.sharding import PartitionSpec as P

LANES = 128
HIGHEST = lax.Precision.HIGHEST


def pieces_of(width):
    for count in (4, 2):
        if width % (count * 256) == 0:
            return count
    return 1


def kernel(
    sizes,
    lengths_in,
    language_in,
    owner_in,
    owner_row_in,
    left_inv_in,
    right_inv_in,
    hidden,
    out_grad,
    proj_in,
    proj_out,
    grads_out,
    means_out,
    hid,
    og,
    w_in,
    w_out,
    part,
    peer_part,
    g_scr,
    pairs,
    gathered,
    places,
    sums,
    counts,
    lengths,
    language,
    owner_list,
    owner_row,
    left_inv,
    right_inv,
    hid_sem,
    og_sem,
    w_sem,
    small_sem,
    t_send,
    t_recv,
    z_send,
    z_recv,
    p_send,
    p_recv,
    m_send,
    m_recv,
):
    t_size, outer, inner, slots = sizes
    seqs, tokens, hid_width = hid.shape
    rank = w_in.shape[0]
    half = rank // t_size
    rows = half // 2
    wide = 2 * rank
    dp = lax.axis_index("dp")
    t_me = lax.axis_index("tensor")
    my_out = dp // inner
    my_in = dp % inner
    hid_pieces = pieces_of(hid_width)
    piece = hid_width // hid_pieces

    def og_copy(s):
        return pltpu.make_async_copy(out_grad.at[s], og.at[s], og_sem.at[s])

    def hid_copy(s, c):
        cols = pl.ds(pl.multiple_of(c * piece, LANES), piece)
        return pltpu.make_async_copy(
            hidden.at[s, :, cols], hid.at[s, :, cols], hid_sem.at[s, c]
        )

    w_in_copy = pltpu.make_async_copy(proj_in, w_in, w_sem.at[0])
    w_out_copy = pltpu.make_async_copy(proj_out, w_out, w_sem.at[1])
    small_copies = [
        pltpu.make_async_copy(source, target, small_sem.at[n])
        for n, (source, target) in enumerate(
            (
                (language_in, language),
                (owner_in, owner_list),
                (owner_row_in, owner_row),
                (lengths_in, lengths),
                (left_inv_in, left_inv),
                (right_inv_in, right_inv),
            )
        )
    ]
    w_out_copy.start()
    og_copy(0).start()
    w_in_copy.start()
    for copy in small_copies:
        copy.start()

    def start_sequence(s):
        def start_piece(c, carry):
            hid_copy(s, c).start()
            return carry

        lax.fori_loop(0, hid_pieces, start_piece, None)

    start_sequence(0)

    def start_later(s, carry):
        og_copy(s).start()
        start_sequence(s)
        return carry

    lax.fori_loop(1, seqs, start_later, None)

    def t_peer(k):
        return (dp, (t_me + k) % t_size)

    def z_peer(k):
        return (((my_out + k) % outer) * inner + my_in, t_me)

    def p_peer(k):
        return (my_out * inner + (my_in + k) % inner, t_me)

    peers = [(t_peer, t_size), (z_peer, outer), (p_peer, inner)]
    barrier = pltpu.get_barrier_semaphore()
    for peer_of, count in peers:
        for k in range(1, count):
            pl.semaphore_signal(
                barrier, inc=1, device_id=peer_of(k), device_id_type=pl.DeviceIdType.MESH
            )

    for copy in small_copies:
        copy.wait()
    own_row = owner_row[...]
    lang_lane = lax.broadcasted_iota(jnp.int32, own_row.shape, 1)
    sub = lax.broadcasted_iota(jnp.int32, places.shape[2:], 0)
    place_block = jnp.full(places.shape[2:], -1, jnp.int32)
    for s in range(seqs):
        lang = language[s]
        own = owner_list[lang]
        earlier = (own_row == own) & (lang_lane < lang)
        slot = jnp.sum(earlier.astype(jnp.int32), axis=1, keepdims=True)
        place_block = jnp.where(sub == s, own * slots + slot, place_block)
    places[my_in, my_out] = place_block
    sums[...] = jnp.zeros_like(sums)
    counts[...] = jnp.zeros_like(counts)

    def send(src, dst, send_sem, recv_sem, peer):
        pltpu.make_async_remote_copy(
            src_ref=src,
            dst_ref=dst,
            send_sem=send_sem,
            recv_sem=recv_sem,
            device_id=peer,
            device_id_type=pl.DeviceIdType.MESH,
        ).start()

    def take(block, sem):
        pltpu.make_async_copy(block, block, sem).wait()

    def project(s):
        og_copy(s).wait()
        dims = (((1,), (1,)), ((), ()))
        right = lax.dot_general(og[s], w_out[...], dims, preferred_element_type=jnp.float32)

        def add_piece(c, left):
            hid_copy(s, c).wait()
            cols = pl.ds(pl.multiple_of(c * piece, LANES), piece)
            return left + lax.dot_general(
                hid[s, :, cols], w_in[:, cols], dims, preferred_element_type=jnp.float32
            )

        left = lax.fori_loop(0, hid_pieces, add_piece, jnp.zeros((tokens, rank), jnp.float32))
        part[s] = jnp.concatenate([left, right], axis=1)
        for k in range(1, t_size):
            send(part.at[s], peer_part.at[s, k - 1], t_send.at[s], t_recv.at[s], t_peer(k))

    first = t_me * half
    even = pl.ds(first, rows, stride=2)
    odd = pl.ds(first + 1, rows, stride=2)

    def reduce(s):
        if t_size > 1:
            take(peer_part.at[s], t_recv.at[s])
        both = part[s]
        for k in range(1, t_size):
            both += peer_part[s, k - 1]
        token = lax.broadcasted_iota(jnp.int32, both.shape, 0)
        both = jnp.where(token < lengths[s], both, 0.0)
        high = both.astype(jnp.bfloat16)
        low = (both - high.astype(jnp.float32)).astype(jnp.bfloat16)
        split = jnp.concatenate([high, low], axis=1)
        full = lax.dot_general(
            split, split, (((0,), (0,)), ((), ())), preferred_element_type=jnp.float32
        )
        full = full[0:rank] + full[wide : wide + rank]
        full = full[:, 0:wide] + full[:, wide : 2 * wide]
        grads = full[:, rank:wide]
        g_scr[...] = grads
        left_rows = jnp.concatenate([left_inv[even, :], left_inv[odd, :]], axis=0)
        done = jnp.dot(left_rows, grads, precision=HIGHEST, preferred_element_type=jnp.float32)
        pre = jnp.dot(
            done, right_inv[...], precision=HIGHEST, preferred_element_type=jnp.float32
        )
        gathered[s, my_in, my_out] = jnp.concatenate([pre[:rows], pre[rows:]], axis=1)
        for k in range(1, outer):
            block = gathered.at[s, my_in, my_out]
            send(block, block, z_send.at[s], z_recv.at[s], z_peer(k))
        pairs[s] = jnp.concatenate([g_scr[even, :], g_scr[odd, :]], axis=1)

    def forward(s):
        @pl.when(s == 0)
        def _():
            if outer > 1:
                take(places.at[0, pl.ds(0, outer - 1)], m_recv.at[0])
            for k in range(1, inner):
                block = places.at[my_in]
                send(block, block, m_send.at[1], m_recv.at[1], p_peer(k))

        if outer > 1:
            take(gathered.at[s, 0, pl.ds(0, outer - 1)], z_recv.at[s])
        for k in range(1, inner):
            block = gathered.at[s, my_in]
            send(block, block, p_send.at[s], p_recv.at[s], p_peer(k))

    def accumulate(s):
        if inner > 1:

            @pl.when(s == 0)
            def _():
                take(places.at[pl.ds(0, inner - 1)], m_recv.at[1])

            take(gathered.at[s, pl.ds(0, inner - 1)], p_recv.at[s])

        def add_block(i, held):
            total, seen = list(held[0]), list(held[1])
            for o in range(outer):
                place = places[i, o, pl.ds(s, 1), :]
                row = gathered[s, i, o]
                for j in range(slots):
                    hit = (place == dp * slots + j).astype(jnp.float32)
                    total[j] = total[j] + hit * row
                    seen[j] = seen[j] + hit
            return tuple(total), tuple(seen)

        total, seen = lax.fori_loop(
            0,
            inner,
            add_block,
            (
                tuple(sums[j] for j in range(slots)),
                tuple(counts[pl.ds(j, 1), :] for j in range(slots)),
            ),
        )
        for j in range(slots):
            sums[j] = total[j]
            counts[pl.ds(j, 1), :] = seen[j]

    w_out_copy.wait()
    w_in_copy.wait()
    pl.semaphore_wait(barrier, sum(count - 1 for _, count in peers))
    for k in range(1, outer):
        block = places.at[my_in, my_out]
        send(block, block, m_send.at[0], m_recv.at[0], z_peer(k))

    def step(i, carry):
        @pl.when(i < seqs)
        def _():
            project(i)

        @pl.when((i >= 1) & (i <= seqs))
        def _():
            reduce(i - 1)

        @pl.when((i >= 2) & (i <= seqs + 1))
        def _():
            forward(i - 2)

        @pl.when(i == seqs + 1)
        def _():
            for s in range(seqs):
                pair = pairs[s]
                for r in range(rows):
                    grads_out[s : s + 1, r * LANES : (r + 1) * LANES] = pair[r : r + 1]

        @pl.when(i >= 3)
        def _():
            accumulate(i - 3)

        return carry

    lax.fori_loop(0, seqs + 3, step, None)
    for j in range(slots):
        mean = sums[j] / jnp.maximum(counts[pl.ds(j, 1), :], 1.0)
        for r in range(rows):
            means_out[j : j + 1, r * LANES : (r + 1) * LANES] = mean[r : r + 1]

    for s in range(seqs):
        if t_size > 1:
            take(peer_part.at[s], t_send.at[s])
        if outer > 1:
            take(gathered.at[s, 0, pl.ds(0, outer - 1)], z_send.at[s])
        if inner > 1:
            take(gathered.at[s, pl.ds(0, inner - 1)], p_send.at[s])
    if outer > 1:
        take(places.at[0, pl.ds(0, outer - 1)], m_send.at[0])
    if inner > 1:
        take(places.at[pl.ds(0, inner - 1)], m_send.at[1])


def per_device(hidden, out_grad, proj_in, proj_out, left_inv, right_inv, lengths, language, owner):
    seqs, tokens, hid_width = hidden.shape
    og_width = out_grad.shape[2]
    rank = proj_in.shape[0]
    t_size = lax.axis_size("tensor")
    dp_size = lax.axis_size("dp")
    inner = 2 ** (int(math.log2(dp_size)) // 2)
    while dp_size % inner:
        inner -= 1
    outer = dp_size // inner
    slots = (owner.shape[0] + dp_size - 1) // dp_size
    half = rank // t_size
    rows = half * rank // LANES
    vmem = pl.BlockSpec(memory_space=pltpu.VMEM)
    anywhere = pl.BlockSpec(memory_space=pl.ANY)
    dma = pltpu.SemaphoreType.DMA
    flops = 2 * seqs * tokens * rank * (hid_width + og_width)
    return pl.pallas_call(
        functools.partial(kernel, (t_size, outer, inner, slots)),
        out_shape=(
            jax.ShapeDtypeStruct((seqs, half * rank), jnp.float32),
            jax.ShapeDtypeStruct((slots, half * rank), jnp.float32),
        ),
        in_specs=[anywhere] * 10,
        out_specs=(vmem, vmem),
        scratch_shapes=[
            pltpu.VMEM((seqs, tokens, hid_width), jnp.bfloat16),
            pltpu.VMEM((seqs, tokens, og_width), jnp.bfloat16),
            pltpu.VMEM((rank, hid_width), jnp.bfloat16),
            pltpu.VMEM((rank, og_width), jnp.bfloat16),
            pltpu.VMEM((seqs, tokens, 2 * rank), jnp.float32),
            pltpu.VMEM((seqs, max(t_size - 1, 1), tokens, 2 * rank), jnp.float32),
            pltpu.VMEM((rank, rank), jnp.float32),
            pltpu.VMEM((seqs, rows, LANES), jnp.float32),
            pltpu.VMEM((seqs, inner, outer, rows, LANES), jnp.float32),
            pltpu.VMEM((inner, outer, 8 * ((seqs + 7) // 8), LANES), jnp.int32),
            pltpu.VMEM((slots, rows, LANES), jnp.float32),
            pltpu.VMEM((8 * ((slots + 7) // 8), LANES), jnp.float32),
            pltpu.SMEM((seqs,), jnp.int32),
            pltpu.SMEM((seqs,), jnp.int32),
            pltpu.SMEM(owner.shape, jnp.int32),
            pltpu.VMEM((1, owner.shape[0]), jnp.int32),
            pltpu.VMEM((rank, rank), jnp.float32),
            pltpu.VMEM((rank, rank), jnp.float32),
            dma((seqs, pieces_of(hid_width))),
            dma((seqs,)),
            dma((2,)),
            dma((6,)),
            dma((seqs,)),
            dma((seqs,)),
            dma((seqs,)),
            dma((seqs,)),
            dma((seqs,)),
            dma((seqs,)),
            dma((2,)),
            dma((2,)),
        ],
        compiler_params=pltpu.CompilerParams(
            collective_id=0, has_side_effects=True, vmem_limit_bytes=64 * 1024 * 1024
        ),
        cost_estimate=pl.CostEstimate(
            flops=flops,
            bytes_accessed=2 * (seqs * tokens + rank) * (hid_width + og_width),
            transcendentals=0,
        ),
    )(
        lengths,
        language,
        owner,
        owner.reshape(1, -1),
        left_inv,
        right_inv,
        hidden,
        out_grad,
        proj_in,
        proj_out,
    )


def solution(mesh):
    return jax.shard_map(
        per_device,
        mesh=mesh,
        in_specs=(
            P("dp", None, "tensor"),
            P("dp", None, "tensor"),
            P(None, "tensor"),
            P(None, "tensor"),
            P(),
            P(),
            P("dp"),
            P("dp"),
            P(),
        ),
        out_specs=(P("dp", "tensor"), P("dp", "tensor")),
        check_vma=False,
    )
```

```python
import functools
import math

import jax
import jax.numpy as jnp
from jax import lax
from jax.experimental import pallas as pl
from jax.experimental.pallas import tpu as pltpu
from jax.sharding import PartitionSpec as P

LANES = 128


def pieces_of(width):
    for count in (4, 2):
        if width % (count * 256) == 0:
            return count
    return 1


def halves(values):
    high = values.astype(jnp.bfloat16)
    return high, (values - high.astype(jnp.float32)).astype(jnp.bfloat16)


def finish(slots, rows_in, grads_out, means_out):
    rows = rows_in.shape[1]
    for n in range(rows_in.shape[0]):
        block = rows_in[n]
        for r in range(rows):
            cols = slice(r * LANES, (r + 1) * LANES)
            if n < slots:
                means_out[n : n + 1, cols] = block[r : r + 1]
            else:
                grads_out[n - slots : n - slots + 1, cols] = block[r : r + 1]


def kernel(
    sizes,
    lengths_in,
    language_in,
    owner_in,
    owner_row_in,
    left_inv_in,
    right_inv_in,
    hidden,
    out_grad,
    proj_in,
    proj_out,
    out,
    hid,
    og,
    w_in,
    w_out,
    part,
    peer_part,
    g_scr,
    l_split,
    r_split,
    gathered,
    places,
    sums,
    counts,
    lengths,
    language,
    owner_list,
    owner_row,
    left_inv,
    right_inv,
    hid_sem,
    og_sem,
    w_sem,
    small_sem,
    t_send,
    t_recv,
    z_send,
    z_recv,
    p_send,
    p_recv,
    m_send,
    m_recv,
):
    t_size, outer, inner, slots = sizes
    seqs, tokens, hid_width = hid.shape
    rank = w_in.shape[0]
    half = rank // t_size
    rows = half // 2
    wide = 2 * rank
    dp = lax.axis_index("dp")
    t_me = lax.axis_index("tensor")
    my_out = dp // inner
    my_in = dp % inner
    hid_pieces = pieces_of(hid_width)
    piece = hid_width // hid_pieces

    def og_copy(s):
        return pltpu.make_async_copy(out_grad.at[s], og.at[s], og_sem.at[s])

    def hid_copy(s, c):
        cols = pl.ds(pl.multiple_of(c * piece, LANES), piece)
        return pltpu.make_async_copy(
            hidden.at[s, :, cols], hid.at[s, :, cols], hid_sem.at[s, c]
        )

    w_in_copy = pltpu.make_async_copy(proj_in, w_in, w_sem.at[0])
    w_out_copy = pltpu.make_async_copy(proj_out, w_out, w_sem.at[1])
    small_copies = [
        pltpu.make_async_copy(source, target, small_sem.at[n])
        for n, (source, target) in enumerate(
            (
                (language_in, language),
                (owner_in, owner_list),
                (owner_row_in, owner_row),
                (lengths_in, lengths),
                (left_inv_in, left_inv),
                (right_inv_in, right_inv),
            )
        )
    ]
    w_out_copy.start()
    og_copy(0).start()
    w_in_copy.start()
    for copy in small_copies:
        copy.start()

    def start_sequence(s):
        def start_piece(c, carry):
            hid_copy(s, c).start()
            return carry

        lax.fori_loop(0, hid_pieces, start_piece, None)

    start_sequence(0)

    def start_later(s, carry):
        og_copy(s).start()
        start_sequence(s)
        return carry

    lax.fori_loop(1, seqs, start_later, None)

    def t_peer(k):
        return (dp, (t_me + k) % t_size)

    def z_peer(k):
        return (((my_out + k) % outer) * inner + my_in, t_me)

    def p_peer(k):
        return (my_out * inner + (my_in + k) % inner, t_me)

    peers = [(t_peer, t_size), (z_peer, outer), (p_peer, inner)]
    barrier = pltpu.get_barrier_semaphore()
    for peer_of, count in peers:
        for k in range(1, count):
            pl.semaphore_signal(
                barrier, inc=1, device_id=peer_of(k), device_id_type=pl.DeviceIdType.MESH
            )

    for copy in small_copies:
        copy.wait()
    own_row = owner_row[...]
    lang_lane = lax.broadcasted_iota(jnp.int32, own_row.shape, 1)
    sub = lax.broadcasted_iota(jnp.int32, places.shape[2:], 0)
    place_block = jnp.full(places.shape[2:], -1, jnp.int32)
    for s in range(seqs):
        lang = language[s]
        own = owner_list[lang]
        earlier = (own_row == own) & (lang_lane < lang)
        slot = jnp.sum(earlier.astype(jnp.int32), axis=1, keepdims=True)
        place_block = jnp.where(sub == s, own * slots + slot, place_block)
    places[my_in, my_out] = place_block
    sums[...] = jnp.zeros_like(sums)
    counts[...] = jnp.zeros_like(counts)

    def send(src, dst, send_sem, recv_sem, peer):
        pltpu.make_async_remote_copy(
            src_ref=src,
            dst_ref=dst,
            send_sem=send_sem,
            recv_sem=recv_sem,
            device_id=peer,
            device_id_type=pl.DeviceIdType.MESH,
        ).start()

    def take(block, sem):
        pltpu.make_async_copy(block, block, sem).wait()

    early = (hid_pieces + 1) // 2

    def project(s, begin, end):
        dims = (((1,), (1,)), ((), ()))

        def add_piece(c, left):
            hid_copy(s, c).wait()
            cols = pl.ds(pl.multiple_of(c * piece, LANES), piece)
            return left + lax.dot_general(
                hid[s, :, cols], w_in[:, cols], dims, preferred_element_type=jnp.float32
            )

        if begin == 0:
            og_copy(s).wait()
            left = jnp.zeros((tokens, rank), jnp.float32)
            right = lax.dot_general(og[s], w_out[...], dims, preferred_element_type=jnp.float32)
            part[s, :, rank:wide] = right
        else:
            left = part[s, :, 0:rank]
        part[s, :, 0:rank] = lax.fori_loop(begin, end, add_piece, left)
        if end == hid_pieces:
            for k in range(1, t_size):
                send(part.at[s], peer_part.at[s, k - 1], t_send.at[s], t_recv.at[s], t_peer(k))

    first = t_me * half
    even = pl.ds(first, rows, stride=2)
    odd = pl.ds(first + 1, rows, stride=2)

    def reduce(s):
        if t_size > 1:
            take(peer_part.at[s], t_recv.at[s])
        both = part[s]
        for k in range(1, t_size):
            both += peer_part[s, k - 1]
        token = lax.broadcasted_iota(jnp.int32, both.shape, 0)
        both = jnp.where(token < lengths[s], both, 0.0)
        high, low = halves(both)
        split = jnp.concatenate([high, low], axis=1)
        full = lax.dot_general(
            split, split, (((0,), (0,)), ((), ())), preferred_element_type=jnp.float32
        )
        full = full[0:rank] + full[wide : wide + rank]
        full = full[:, 0:wide] + full[:, wide : 2 * wide]
        grads = full[:, rank:wide]
        g_scr[...] = grads
        high, low = halves(grads)
        done = jnp.dot(
            l_split[...],
            jnp.concatenate([high, low, high], axis=0),
            preferred_element_type=jnp.float32,
        )
        high, low = halves(done)
        pre = jnp.dot(
            jnp.concatenate([high, low, high], axis=1),
            r_split[...],
            preferred_element_type=jnp.float32,
        )
        gathered[s, my_in, my_out] = jnp.concatenate([pre[:rows], pre[rows:]], axis=1)
        for k in range(1, outer):
            block = gathered.at[s, my_in, my_out]
            send(block, block, z_send.at[s], z_recv.at[s], z_peer(k))
        out[slots + s] = jnp.concatenate([g_scr[even, :], g_scr[odd, :]], axis=1)

    def forward(s):
        @pl.when(s == 0)
        def _():
            if outer > 1:
                take(places.at[0, pl.ds(0, outer - 1)], m_recv.at[0])
            for k in range(1, inner):
                block = places.at[my_in]
                send(block, block, m_send.at[1], m_recv.at[1], p_peer(k))

        if outer > 1:
            take(gathered.at[s, 0, pl.ds(0, outer - 1)], z_recv.at[s])
        for k in range(1, inner):
            block = gathered.at[s, my_in]
            send(block, block, p_send.at[s], p_recv.at[s], p_peer(k))

    def accumulate(s):
        if inner > 1:

            @pl.when(s == 0)
            def _():
                take(places.at[pl.ds(0, inner - 1)], m_recv.at[1])

            take(gathered.at[s, pl.ds(0, inner - 1)], p_recv.at[s])

        def add_block(i, held):
            total, seen = list(held[0]), list(held[1])
            for o in range(outer):
                place = places[i, o, pl.ds(s, 1), :]
                row = gathered[s, i, o]
                for j in range(slots):
                    hit = (place == dp * slots + j).astype(jnp.float32)
                    total[j] = total[j] + hit * row
                    seen[j] = seen[j] + hit
            return tuple(total), tuple(seen)

        total, seen = lax.fori_loop(
            0,
            inner,
            add_block,
            (
                tuple(sums[j] for j in range(slots)),
                tuple(counts[pl.ds(j, 1), :] for j in range(slots)),
            ),
        )
        for j in range(slots):
            sums[j] = total[j]
            counts[pl.ds(j, 1), :] = seen[j]

    w_out_copy.wait()
    w_in_copy.wait()
    pl.semaphore_wait(barrier, sum(count - 1 for _, count in peers))
    for k in range(1, outer):
        block = places.at[my_in, my_out]
        send(block, block, m_send.at[0], m_recv.at[0], z_peer(k))

    left_rows = jnp.concatenate([left_inv[even, :], left_inv[odd, :]], axis=0)
    high, low = halves(left_rows)
    l_split[...] = jnp.concatenate([high, high, low], axis=1)
    high, low = halves(right_inv[...])
    r_split[...] = jnp.concatenate([high, high, low], axis=0)

    def step(i, carry):
        @pl.when(i < seqs)
        def _():
            project(i, 0, early)

        @pl.when((i >= 1) & (i <= seqs))
        def _():
            reduce(i - 1)

        if early < hid_pieces:

            @pl.when(i < seqs)
            def _():
                project(i, early, hid_pieces)

        @pl.when((i >= 1) & (i <= seqs))
        def _():
            forward(i - 1)

        @pl.when(i >= 2)
        def _():
            accumulate(i - 2)

        return carry

    lax.fori_loop(0, seqs + 2, step, None)
    for j in range(slots):
        out[j] = sums[j] / jnp.maximum(counts[pl.ds(j, 1), :], 1.0)

    for s in range(seqs):
        if t_size > 1:
            take(peer_part.at[s], t_send.at[s])
        if outer > 1:
            take(gathered.at[s, 0, pl.ds(0, outer - 1)], z_send.at[s])
        if inner > 1:
            take(gathered.at[s, pl.ds(0, inner - 1)], p_send.at[s])
    if outer > 1:
        take(places.at[0, pl.ds(0, outer - 1)], m_send.at[0])
    if inner > 1:
        take(places.at[pl.ds(0, inner - 1)], m_send.at[1])


def per_device(hidden, out_grad, proj_in, proj_out, left_inv, right_inv, lengths, language, owner):
    seqs, tokens, hid_width = hidden.shape
    og_width = out_grad.shape[2]
    rank = proj_in.shape[0]
    t_size = lax.axis_size("tensor")
    dp_size = lax.axis_size("dp")
    inner = 2 ** (int(math.log2(dp_size)) // 2)
    while dp_size % inner:
        inner -= 1
    outer = dp_size // inner
    slots = (owner.shape[0] + dp_size - 1) // dp_size
    half = rank // t_size
    rows = half * rank // LANES
    vmem = pl.BlockSpec(memory_space=pltpu.VMEM)
    anywhere = pl.BlockSpec(memory_space=pl.ANY)
    dma = pltpu.SemaphoreType.DMA
    flops = 2 * seqs * tokens * rank * (hid_width + og_width)
    blocks = pl.pallas_call(
        functools.partial(kernel, (t_size, outer, inner, slots)),
        out_shape=jax.ShapeDtypeStruct((slots + seqs, rows, LANES), jnp.float32),
        in_specs=[anywhere] * 10,
        out_specs=vmem,
        scratch_shapes=[
            pltpu.VMEM((seqs, tokens, hid_width), jnp.bfloat16),
            pltpu.VMEM((seqs, tokens, og_width), jnp.bfloat16),
            pltpu.VMEM((rank, hid_width), jnp.bfloat16),
            pltpu.VMEM((rank, og_width), jnp.bfloat16),
            pltpu.VMEM((seqs, tokens, 2 * rank), jnp.float32),
            pltpu.VMEM((seqs, max(t_size - 1, 1), tokens, 2 * rank), jnp.float32),
            pltpu.VMEM((rank, rank), jnp.float32),
            pltpu.VMEM((half, 3 * rank), jnp.bfloat16),
            pltpu.VMEM((3 * rank, rank), jnp.bfloat16),
            pltpu.VMEM((seqs, inner, outer, rows, LANES), jnp.float32),
            pltpu.VMEM((inner, outer, 8 * ((seqs + 7) // 8), LANES), jnp.int32),
            pltpu.VMEM((slots, rows, LANES), jnp.float32),
            pltpu.VMEM((8 * ((slots + 7) // 8), LANES), jnp.float32),
            pltpu.SMEM((seqs,), jnp.int32),
            pltpu.SMEM((seqs,), jnp.int32),
            pltpu.SMEM(owner.shape, jnp.int32),
            pltpu.VMEM((1, owner.shape[0]), jnp.int32),
            pltpu.VMEM((rank, rank), jnp.float32),
            pltpu.VMEM((rank, rank), jnp.float32),
            dma((seqs, pieces_of(hid_width))),
            dma((seqs,)),
            dma((2,)),
            dma((6,)),
            dma((seqs,)),
            dma((seqs,)),
            dma((seqs,)),
            dma((seqs,)),
            dma((seqs,)),
            dma((seqs,)),
            dma((2,)),
            dma((2,)),
        ],
        compiler_params=pltpu.CompilerParams(
            collective_id=0, has_side_effects=True, vmem_limit_bytes=64 * 1024 * 1024
        ),
        cost_estimate=pl.CostEstimate(
            flops=flops,
            bytes_accessed=2 * (seqs * tokens + rank) * (hid_width + og_width),
            transcendentals=0,
        ),
    )(
        lengths,
        language,
        owner,
        owner.reshape(1, -1),
        left_inv,
        right_inv,
        hidden,
        out_grad,
        proj_in,
        proj_out,
    )
    return pl.pallas_call(
        functools.partial(finish, slots),
        out_shape=(
            jax.ShapeDtypeStruct((seqs, half * rank), jnp.float32),
            jax.ShapeDtypeStruct((slots, half * rank), jnp.float32),
        ),
        in_specs=[vmem],
        out_specs=(vmem, vmem),
    )(blocks)


def solution(mesh):
    return jax.shard_map(
        per_device,
        mesh=mesh,
        in_specs=(
            P("dp", None, "tensor"),
            P("dp", None, "tensor"),
            P(None, "tensor"),
            P(None, "tensor"),
            P(),
            P(),
            P("dp"),
            P("dp"),
            P(),
        ),
        out_specs=(P("dp", "tensor"), P("dp", "tensor")),
        check_vma=False,
    )
```

```python
import functools
import math

import jax
import jax.numpy as jnp
from jax import lax
from jax.experimental import pallas as pl
from jax.experimental.pallas import tpu as pltpu
from jax.sharding import PartitionSpec as P

LANES = 128


def pieces_of(width):
    for count in (4, 2):
        if width % (count * 256) == 0:
            return count
    return 1


def halves(values):
    high = values.astype(jnp.bfloat16)
    return high, (values - high.astype(jnp.float32)).astype(jnp.bfloat16)


def finish(slots, rows_in, grads_out, means_out):
    rows = rows_in.shape[1]
    for n in range(rows_in.shape[0]):
        block = rows_in[n]
        for r in range(rows):
            cols = slice(r * LANES, (r + 1) * LANES)
            if n < slots:
                means_out[n : n + 1, cols] = block[r : r + 1]
            else:
                grads_out[n - slots : n - slots + 1, cols] = block[r : r + 1]


def kernel(
    sizes,
    lengths_in,
    language_in,
    owner_in,
    owner_row_in,
    left_inv_in,
    right_inv_in,
    hidden,
    out_grad,
    proj_in,
    proj_out,
    out,
    hid,
    og,
    w_in,
    w_out,
    part,
    peer_part,
    g_scr,
    l_split,
    r_split,
    gathered,
    places,
    sums,
    counts,
    lengths,
    language,
    owner_list,
    owner_row,
    left_inv,
    right_inv,
    hid_sem,
    og_sem,
    w_sem,
    small_sem,
    t_send,
    t_recv,
    z_send,
    z_recv,
    p_send,
    p_recv,
    m_send,
    m_recv,
):
    t_size, outer, inner, slots = sizes
    seqs, tokens, hid_width = hid.shape
    rank = w_in.shape[0]
    half = rank // t_size
    rows = half // 2
    wide = 2 * rank
    dp = lax.axis_index("dp")
    t_me = lax.axis_index("tensor")
    my_out = dp // inner
    my_in = dp % inner
    hid_pieces = pieces_of(hid_width)
    piece = hid_width // hid_pieces
    cut = 256 * ((piece // 256 + 1) // 2)

    def og_copy(s):
        return pltpu.make_async_copy(out_grad.at[s], og.at[s], og_sem.at[s])

    def hid_copy(s, c):
        cols = pl.ds(pl.multiple_of(c * piece, LANES), piece)
        return pltpu.make_async_copy(
            hidden.at[s, :, cols], hid.at[s, :, cols], hid_sem.at[s, c]
        )

    w_in_copy = pltpu.make_async_copy(proj_in, w_in, w_sem.at[0])
    w_out_copy = pltpu.make_async_copy(proj_out, w_out, w_sem.at[1])
    small_copies = [
        pltpu.make_async_copy(source, target, small_sem.at[n])
        for n, (source, target) in enumerate(
            (
                (language_in, language),
                (owner_in, owner_list),
                (owner_row_in, owner_row),
                (lengths_in, lengths),
                (left_inv_in, left_inv),
                (right_inv_in, right_inv),
            )
        )
    ]
    w_out_copy.start()
    og_copy(0).start()
    w_in_copy.start()
    for copy in small_copies:
        copy.start()

    def start_piece(c, carry):
        hid_copy(0, c).start()
        return carry

    lax.fori_loop(0, hid_pieces, start_piece, None)

    def t_peer(k):
        return (dp, (t_me + k) % t_size)

    def z_peer(k):
        return (((my_out + k) % outer) * inner + my_in, t_me)

    def p_peer(k):
        return (my_out * inner + (my_in + k) % inner, t_me)

    peers = [(t_peer, t_size), (z_peer, outer), (p_peer, inner)]
    barrier = pltpu.get_barrier_semaphore()
    for peer_of, count in peers:
        for k in range(1, count):
            pl.semaphore_signal(
                barrier, inc=1, device_id=peer_of(k), device_id_type=pl.DeviceIdType.MESH
            )

    for copy in small_copies:
        copy.wait()
    own_row = owner_row[...]
    lang_lane = lax.broadcasted_iota(jnp.int32, own_row.shape, 1)
    sub = lax.broadcasted_iota(jnp.int32, places.shape[2:], 0)
    place_block = jnp.full(places.shape[2:], -1, jnp.int32)
    for s in range(seqs):
        lang = language[s]
        own = owner_list[lang]
        earlier = (own_row == own) & (lang_lane < lang)
        slot = jnp.sum(earlier.astype(jnp.int32), axis=1, keepdims=True)
        place_block = jnp.where(sub == s, own * slots + slot, place_block)
    places[my_in, my_out] = place_block
    sums[...] = jnp.zeros_like(sums)
    counts[...] = jnp.zeros_like(counts)

    def send(src, dst, send_sem, recv_sem, peer):
        pltpu.make_async_remote_copy(
            src_ref=src,
            dst_ref=dst,
            send_sem=send_sem,
            recv_sem=recv_sem,
            device_id=peer,
            device_id_type=pl.DeviceIdType.MESH,
        ).start()

    def take(block, sem):
        pltpu.make_async_copy(block, block, sem).wait()

    def project(s):
        dims = (((1,), (1,)), ((), ()))
        og_copy(s).wait()

        @pl.when(s + 1 < seqs)
        def _():
            og_copy(s + 1).start()

        right = lax.dot_general(og[s], w_out[...], dims, preferred_element_type=jnp.float32)
        part[s, :, rank:wide] = right

        def add_piece(c, left):
            hid_copy(s, c).wait()

            @pl.when(s + 1 < seqs)
            def _():
                hid_copy(s + 1, c).start()

            base = pl.multiple_of(c * piece, LANES)
            for begin, end in ((0, cut), (cut, piece)):
                cols = pl.ds(base + begin, end - begin)
                left += lax.dot_general(
                    hid[s, :, cols], w_in[:, cols], dims, preferred_element_type=jnp.float32
                )
            return left

        part[s, :, 0:rank] = lax.fori_loop(
            0, hid_pieces, add_piece, jnp.zeros((tokens, rank), jnp.float32)
        )
        for k in range(1, t_size):
            send(part.at[s], peer_part.at[s, k - 1], t_send.at[s], t_recv.at[s], t_peer(k))

    first = t_me * half
    even = pl.ds(first, rows, stride=2)
    odd = pl.ds(first + 1, rows, stride=2)

    def reduce(s):
        if t_size > 1:
            take(peer_part.at[s], t_recv.at[s])
        both = part[s]
        for k in range(1, t_size):
            both += peer_part[s, k - 1]
        token = lax.broadcasted_iota(jnp.int32, both.shape, 0)
        both = jnp.where(token < lengths[s], both, 0.0)
        high, low = halves(both)
        split = jnp.concatenate([high, low], axis=1)
        full = lax.dot_general(
            split, split, (((0,), (0,)), ((), ())), preferred_element_type=jnp.float32
        )
        full = full[0:rank] + full[wide : wide + rank]
        full = full[:, 0:wide] + full[:, wide : 2 * wide]
        grads = full[:, rank:wide]
        g_scr[...] = grads
        high, low = halves(grads)
        done = jnp.dot(
            l_split[...],
            jnp.concatenate([high, low, high], axis=0),
            preferred_element_type=jnp.float32,
        )
        high, low = halves(done)
        pre = jnp.dot(
            jnp.concatenate([high, low, high], axis=1),
            r_split[...],
            preferred_element_type=jnp.float32,
        )
        gathered[s, my_in, my_out] = jnp.concatenate([pre[:rows], pre[rows:]], axis=1)
        for k in range(1, outer):
            block = gathered.at[s, my_in, my_out]
            send(block, block, z_send.at[s], z_recv.at[s], z_peer(k))
        out[slots + s] = jnp.concatenate([g_scr[even, :], g_scr[odd, :]], axis=1)

    def forward(s):
        @pl.when(s == 0)
        def _():
            if outer > 1:
                take(places.at[0, pl.ds(0, outer - 1)], m_recv.at[0])
            for k in range(1, inner):
                block = places.at[my_in]
                send(block, block, m_send.at[1], m_recv.at[1], p_peer(k))

        if outer > 1:
            take(gathered.at[s, 0, pl.ds(0, outer - 1)], z_recv.at[s])
        for k in range(1, inner):
            block = gathered.at[s, my_in]
            send(block, block, p_send.at[s], p_recv.at[s], p_peer(k))

    def accumulate(s):
        if inner > 1:

            @pl.when(s == 0)
            def _():
                take(places.at[pl.ds(0, inner - 1)], m_recv.at[1])

            take(gathered.at[s, pl.ds(0, inner - 1)], p_recv.at[s])

        def add_block(i, held):
            total, seen = list(held[0]), list(held[1])
            for o in range(outer):
                place = places[i, o, pl.ds(s, 1), :]
                row = gathered[s, i, o]
                for j in range(slots):
                    hit = (place == dp * slots + j).astype(jnp.float32)
                    total[j] = total[j] + hit * row
                    seen[j] = seen[j] + hit
            return tuple(total), tuple(seen)

        total, seen = lax.fori_loop(
            0,
            inner,
            add_block,
            (
                tuple(sums[j] for j in range(slots)),
                tuple(counts[pl.ds(j, 1), :] for j in range(slots)),
            ),
        )
        for j in range(slots):
            sums[j] = total[j]
            counts[pl.ds(j, 1), :] = seen[j]

    w_out_copy.wait()
    w_in_copy.wait()
    pl.semaphore_wait(barrier, sum(count - 1 for _, count in peers))
    for k in range(1, outer):
        block = places.at[my_in, my_out]
        send(block, block, m_send.at[0], m_recv.at[0], z_peer(k))

    left_rows = jnp.concatenate([left_inv[even, :], left_inv[odd, :]], axis=0)
    high, low = halves(left_rows)
    l_split[...] = jnp.concatenate([high, high, low], axis=1)
    high, low = halves(right_inv[...])
    r_split[...] = jnp.concatenate([high, high, low], axis=0)

    def step(i, carry):
        @pl.when(i < seqs)
        def _():
            project(i)

        @pl.when((i >= 1) & (i <= seqs))
        def _():
            reduce(i - 1)

        @pl.when((i >= 2) & (i <= seqs + 1))
        def _():
            forward(i - 2)

        @pl.when(i >= 3)
        def _():
            accumulate(i - 3)

        return carry

    lax.fori_loop(0, seqs + 3, step, None)
    for j in range(slots):
        out[j] = sums[j] / jnp.maximum(counts[pl.ds(j, 1), :], 1.0)

    for s in range(seqs):
        if t_size > 1:
            take(peer_part.at[s], t_send.at[s])
        if outer > 1:
            take(gathered.at[s, 0, pl.ds(0, outer - 1)], z_send.at[s])
        if inner > 1:
            take(gathered.at[s, pl.ds(0, inner - 1)], p_send.at[s])
    if outer > 1:
        take(places.at[0, pl.ds(0, outer - 1)], m_send.at[0])
    if inner > 1:
        take(places.at[pl.ds(0, inner - 1)], m_send.at[1])


def per_device(hidden, out_grad, proj_in, proj_out, left_inv, right_inv, lengths, language, owner):
    seqs, tokens, hid_width = hidden.shape
    og_width = out_grad.shape[2]
    rank = proj_in.shape[0]
    t_size = lax.axis_size("tensor")
    dp_size = lax.axis_size("dp")
    inner = 2 ** (int(math.log2(dp_size)) // 2)
    while dp_size % inner:
        inner -= 1
    outer = dp_size // inner
    slots = (owner.shape[0] + dp_size - 1) // dp_size
    half = rank // t_size
    rows = half * rank // LANES
    vmem = pl.BlockSpec(memory_space=pltpu.VMEM)
    anywhere = pl.BlockSpec(memory_space=pl.ANY)
    dma = pltpu.SemaphoreType.DMA
    flops = 2 * seqs * tokens * rank * (hid_width + og_width)
    blocks = pl.pallas_call(
        functools.partial(kernel, (t_size, outer, inner, slots)),
        out_shape=jax.ShapeDtypeStruct((slots + seqs, rows, LANES), jnp.float32),
        in_specs=[anywhere] * 10,
        out_specs=vmem,
        scratch_shapes=[
            pltpu.VMEM((seqs, tokens, hid_width), jnp.bfloat16),
            pltpu.VMEM((seqs, tokens, og_width), jnp.bfloat16),
            pltpu.VMEM((rank, hid_width), jnp.bfloat16),
            pltpu.VMEM((rank, og_width), jnp.bfloat16),
            pltpu.VMEM((seqs, tokens, 2 * rank), jnp.float32),
            pltpu.VMEM((seqs, max(t_size - 1, 1), tokens, 2 * rank), jnp.float32),
            pltpu.VMEM((rank, rank), jnp.float32),
            pltpu.VMEM((half, 3 * rank), jnp.bfloat16),
            pltpu.VMEM((3 * rank, rank), jnp.bfloat16),
            pltpu.VMEM((seqs, inner, outer, rows, LANES), jnp.float32),
            pltpu.VMEM((inner, outer, 8 * ((seqs + 7) // 8), LANES), jnp.int32),
            pltpu.VMEM((slots, rows, LANES), jnp.float32),
            pltpu.VMEM((8 * ((slots + 7) // 8), LANES), jnp.float32),
            pltpu.SMEM((seqs,), jnp.int32),
            pltpu.SMEM((seqs,), jnp.int32),
            pltpu.SMEM(owner.shape, jnp.int32),
            pltpu.VMEM((1, owner.shape[0]), jnp.int32),
            pltpu.VMEM((rank, rank), jnp.float32),
            pltpu.VMEM((rank, rank), jnp.float32),
            dma((seqs, pieces_of(hid_width))),
            dma((seqs,)),
            dma((2,)),
            dma((6,)),
            dma((seqs,)),
            dma((seqs,)),
            dma((seqs,)),
            dma((seqs,)),
            dma((seqs,)),
            dma((seqs,)),
            dma((2,)),
            dma((2,)),
        ],
        compiler_params=pltpu.CompilerParams(
            collective_id=0, has_side_effects=True, vmem_limit_bytes=64 * 1024 * 1024
        ),
        cost_estimate=pl.CostEstimate(
            flops=flops,
            bytes_accessed=2 * (seqs * tokens + rank) * (hid_width + og_width),
            transcendentals=0,
        ),
    )(
        lengths,
        language,
        owner,
        owner.reshape(1, -1),
        left_inv,
        right_inv,
        hidden,
        out_grad,
        proj_in,
        proj_out,
    )
    return pl.pallas_call(
        functools.partial(finish, slots),
        out_shape=(
            jax.ShapeDtypeStruct((seqs, half * rank), jnp.float32),
            jax.ShapeDtypeStruct((slots, half * rank), jnp.float32),
        ),
        in_specs=[vmem],
        out_specs=(vmem, vmem),
    )(blocks)


def solution(mesh):
    return jax.shard_map(
        per_device,
        mesh=mesh,
        in_specs=(
            P("dp", None, "tensor"),
            P("dp", None, "tensor"),
            P(None, "tensor"),
            P(None, "tensor"),
            P(),
            P(),
            P("dp"),
            P("dp"),
            P(),
        ),
        out_specs=(P("dp", "tensor"), P("dp", "tensor")),
        check_vma=False,
    )
```

```python
import functools
import math

import jax
import jax.numpy as jnp
from jax import lax
from jax.experimental import pallas as pl
from jax.experimental.pallas import tpu as pltpu
from jax.sharding import PartitionSpec as P

LANES = 128


def pieces_of(width):
    for count in (4, 2):
        if width % (count * 256) == 0:
            return count
    return 1


def halves(values):
    high = values.astype(jnp.bfloat16)
    return high, (values - high.astype(jnp.float32)).astype(jnp.bfloat16)


def finish(slots, rows_in, grads_out, means_out):
    rows = rows_in.shape[1]
    for n in range(rows_in.shape[0]):
        block = rows_in[n]
        for r in range(rows):
            cols = slice(r * LANES, (r + 1) * LANES)
            if n < slots:
                means_out[n : n + 1, cols] = block[r : r + 1]
            else:
                grads_out[n - slots : n - slots + 1, cols] = block[r : r + 1]


def kernel(
    sizes,
    lengths_in,
    language_in,
    owner_in,
    owner_row_in,
    left_inv_in,
    right_inv_in,
    hidden,
    out_grad,
    proj_in,
    proj_out,
    out,
    hid,
    og,
    w_in,
    w_out,
    part,
    peer_part,
    g_scr,
    l_split,
    r_split,
    gathered,
    places,
    sums,
    counts,
    lengths,
    language,
    owner_list,
    owner_row,
    left_inv,
    right_inv,
    hid_sem,
    og_sem,
    w_sem,
    small_sem,
    t_send,
    t_recv,
    z_send,
    z_recv,
    p_send,
    p_recv,
    d_send,
    d_recv,
    m_send,
    m_recv,
):
    t_size, outer, inner, slots = sizes
    seqs, tokens, hid_width = hid.shape
    rank = w_in.shape[0]
    half = rank // t_size
    rows = half // 2
    wide = 2 * rank
    dp = lax.axis_index("dp")
    t_me = lax.axis_index("tensor")
    my_out = dp // inner
    my_in = dp % inner
    me = my_in * outer + my_out
    last = seqs - 1
    hid_pieces = pieces_of(hid_width)
    piece = hid_width // hid_pieces
    cut = 256 * ((piece // 256 + 1) // 2)

    def og_copy(s):
        return pltpu.make_async_copy(out_grad.at[s], og.at[s], og_sem.at[s])

    def hid_copy(s, c):
        cols = pl.ds(pl.multiple_of(c * piece, LANES), piece)
        return pltpu.make_async_copy(
            hidden.at[s, :, cols], hid.at[s, :, cols], hid_sem.at[s, c]
        )

    w_in_copy = pltpu.make_async_copy(proj_in, w_in, w_sem.at[0])
    w_out_copy = pltpu.make_async_copy(proj_out, w_out, w_sem.at[1])
    small_copies = [
        pltpu.make_async_copy(source, target, small_sem.at[n])
        for n, (source, target) in enumerate(
            (
                (language_in, language),
                (owner_in, owner_list),
                (owner_row_in, owner_row),
                (lengths_in, lengths),
                (left_inv_in, left_inv),
                (right_inv_in, right_inv),
            )
        )
    ]
    w_out_copy.start()
    og_copy(0).start()
    w_in_copy.start()
    for copy in small_copies:
        copy.start()

    def start_piece(c, carry):
        hid_copy(0, c).start()
        return carry

    lax.fori_loop(0, hid_pieces, start_piece, None)

    def t_peer(k):
        return (dp, (t_me + k) % t_size)

    def z_peer(k):
        return (((my_out + k) % outer) * inner + my_in, t_me)

    def p_peer(k):
        return (my_out * inner + (my_in + k) % inner, t_me)

    others = outer * inner - 1

    def each_other(act):
        def visit(n, carry):
            act(((dp + 1 + (n + others // 2) % others) % (others + 1), t_me))
            return carry

        if others:
            lax.fori_loop(0, others, visit, None)

    barrier = pltpu.get_barrier_semaphore()

    def greet(peer):
        pl.semaphore_signal(
            barrier, inc=1, device_id=peer, device_id_type=pl.DeviceIdType.MESH
        )

    for k in range(1, t_size):
        greet(t_peer(k))
    each_other(greet)

    for copy in small_copies:
        copy.wait()
    own_row = owner_row[...]
    lang_lane = lax.broadcasted_iota(jnp.int32, own_row.shape, 1)
    sub = lax.broadcasted_iota(jnp.int32, places.shape[1:], 0)
    place_block = jnp.full(places.shape[1:], -1, jnp.int32)
    for s in range(seqs):
        lang = language[s]
        own = owner_list[lang]
        earlier = (own_row == own) & (lang_lane < lang)
        slot = jnp.sum(earlier.astype(jnp.int32), axis=1, keepdims=True)
        place_block = jnp.where(sub == s, own * slots + slot, place_block)
    places[me] = place_block
    sums[...] = jnp.zeros_like(sums)
    counts[...] = jnp.zeros_like(counts)

    def send(src, dst, send_sem, recv_sem, peer):
        pltpu.make_async_remote_copy(
            src_ref=src,
            dst_ref=dst,
            send_sem=send_sem,
            recv_sem=recv_sem,
            device_id=peer,
            device_id_type=pl.DeviceIdType.MESH,
        ).start()

    def take(block, sem):
        pltpu.make_async_copy(block, block, sem).wait()

    def project(s):
        dims = (((1,), (1,)), ((), ()))
        og_copy(s).wait()

        @pl.when(s + 1 < seqs)
        def _():
            og_copy(s + 1).start()

        right = lax.dot_general(og[s], w_out[...], dims, preferred_element_type=jnp.float32)
        part[s, :, rank:wide] = right

        def add_piece(c, left):
            hid_copy(s, c).wait()

            @pl.when(s + 1 < seqs)
            def _():
                hid_copy(s + 1, c).start()

            base = pl.multiple_of(c * piece, LANES)
            for begin, end in ((0, cut), (cut, piece)):
                cols = pl.ds(base + begin, end - begin)
                left += lax.dot_general(
                    hid[s, :, cols], w_in[:, cols], dims, preferred_element_type=jnp.float32
                )
            return left

        part[s, :, 0:rank] = lax.fori_loop(
            0, hid_pieces, add_piece, jnp.zeros((tokens, rank), jnp.float32)
        )
        for k in range(1, t_size):
            for q in range(4):
                some = pl.ds(q * (tokens // 4), tokens // 4)
                send(
                    part.at[s, some],
                    peer_part.at[s, k - 1, some],
                    t_send.at[s],
                    t_recv.at[s],
                    t_peer(k),
                )

    first = t_me * half
    even = pl.ds(first, rows, stride=2)
    odd = pl.ds(first + 1, rows, stride=2)

    def reduce(s):
        if t_size > 1:
            take(peer_part.at[s], t_recv.at[s])
        both = part[s]
        for k in range(1, t_size):
            both += peer_part[s, k - 1]
        token = lax.broadcasted_iota(jnp.int32, both.shape, 0)
        both = jnp.where(token < lengths[s], both, 0.0)
        high, low = halves(both)
        split = jnp.concatenate([high, low], axis=1)
        full = lax.dot_general(
            split, split, (((0,), (0,)), ((), ())), preferred_element_type=jnp.float32
        )
        full = full[0:rank] + full[wide : wide + rank]
        full = full[:, 0:wide] + full[:, wide : 2 * wide]
        grads = full[:, rank:wide]
        g_scr[...] = grads
        high, low = halves(grads)
        done = jnp.dot(
            l_split[...],
            jnp.concatenate([high, low, high], axis=0),
            preferred_element_type=jnp.float32,
        )
        high, low = halves(done)
        pre = jnp.dot(
            jnp.concatenate([high, low, high], axis=1),
            r_split[...],
            preferred_element_type=jnp.float32,
        )
        gathered[s, me] = jnp.concatenate([pre[:rows], pre[rows:]], axis=1)
        block = gathered.at[s, me]

        @pl.when(s < last)
        def _():
            for k in range(1, outer):
                send(block, block, z_send.at[s], z_recv.at[s], z_peer(k))

        @pl.when(s == last)
        def _():
            each_other(lambda peer: send(block, block, d_send.at[0], d_recv.at[0], peer))

        out[slots + s] = jnp.concatenate([g_scr[even, :], g_scr[odd, :]], axis=1)

    def forward(s):
        if outer > 1:
            take(gathered.at[s, pl.ds(0, outer - 1)], z_recv.at[s])
        block = gathered.at[s, pl.ds(my_in * outer, outer)]
        for k in range(1, inner):
            send(block, block, p_send.at[s], p_recv.at[s], p_peer(k))

    def accumulate(s):
        if others:

            @pl.when(s == 0)
            def _():
                take(places.at[pl.ds(0, others)], m_recv.at[0])

            @pl.when(s == last)
            def _():
                take(gathered.at[last, pl.ds(0, others)], d_recv.at[0])

        if inner > 1:

            @pl.when(s < last)
            def _():
                take(gathered.at[s, pl.ds(0, (inner - 1) * outer)], p_recv.at[s])

        def add_block(i, held):
            total, seen = list(held[0]), list(held[1])
            for o in range(outer):
                place = places[i * outer + o, pl.ds(s, 1), :]
                row = gathered[s, i * outer + o]
                for j in range(slots):
                    hit = (place == dp * slots + j).astype(jnp.float32)
                    total[j] = total[j] + hit * row
                    seen[j] = seen[j] + hit
            return tuple(total), tuple(seen)

        total, seen = lax.fori_loop(
            0,
            inner,
            add_block,
            (
                tuple(sums[j] for j in range(slots)),
                tuple(counts[pl.ds(j, 1), :] for j in range(slots)),
            ),
        )
        for j in range(slots):
            sums[j] = total[j]
            counts[pl.ds(j, 1), :] = seen[j]

    w_out_copy.wait()
    w_in_copy.wait()
    pl.semaphore_wait(barrier, t_size - 1 + others)
    own_places = places.at[me]
    each_other(lambda peer: send(own_places, own_places, m_send.at[0], m_recv.at[0], peer))

    left_rows = jnp.concatenate([left_inv[even, :], left_inv[odd, :]], axis=0)
    high, low = halves(left_rows)
    l_split[...] = jnp.concatenate([high, high, low], axis=1)
    high, low = halves(right_inv[...])
    r_split[...] = jnp.concatenate([high, high, low], axis=0)

    def step(i, carry):
        @pl.when(i < seqs)
        def _():
            project(i)

        @pl.when((i >= 1) & (i <= seqs))
        def _():
            reduce(i - 1)

        @pl.when((i >= 2) & (i <= seqs))
        def _():
            forward(i - 2)

        @pl.when(i >= 3)
        def _():
            accumulate(i - 3)

        return carry

    lax.fori_loop(0, seqs + 3, step, None)
    for j in range(slots):
        out[j] = sums[j] / jnp.maximum(counts[pl.ds(j, 1), :], 1.0)

    for s in range(seqs):
        if t_size > 1:
            take(peer_part.at[s], t_send.at[s])
    for s in range(last):
        if outer > 1:
            take(gathered.at[s, pl.ds(0, outer - 1)], z_send.at[s])
        if inner > 1:
            take(gathered.at[s, pl.ds(0, (inner - 1) * outer)], p_send.at[s])
    if others:
        take(gathered.at[last, pl.ds(0, others)], d_send.at[0])
        take(places.at[pl.ds(0, others)], m_send.at[0])


def per_device(hidden, out_grad, proj_in, proj_out, left_inv, right_inv, lengths, language, owner):
    seqs, tokens, hid_width = hidden.shape
    og_width = out_grad.shape[2]
    rank = proj_in.shape[0]
    t_size = lax.axis_size("tensor")
    dp_size = lax.axis_size("dp")
    inner = 2 ** (int(math.log2(dp_size)) // 2)
    while dp_size % inner:
        inner -= 1
    outer = dp_size // inner
    slots = (owner.shape[0] + dp_size - 1) // dp_size
    half = rank // t_size
    rows = half * rank // LANES
    vmem = pl.BlockSpec(memory_space=pltpu.VMEM)
    anywhere = pl.BlockSpec(memory_space=pl.ANY)
    dma = pltpu.SemaphoreType.DMA
    flops = 2 * seqs * tokens * rank * (hid_width + og_width)
    blocks = pl.pallas_call(
        functools.partial(kernel, (t_size, outer, inner, slots)),
        out_shape=jax.ShapeDtypeStruct((slots + seqs, rows, LANES), jnp.float32),
        in_specs=[anywhere] * 10,
        out_specs=vmem,
        scratch_shapes=[
            pltpu.VMEM((seqs, tokens, hid_width), jnp.bfloat16),
            pltpu.VMEM((seqs, tokens, og_width), jnp.bfloat16),
            pltpu.VMEM((rank, hid_width), jnp.bfloat16),
            pltpu.VMEM((rank, og_width), jnp.bfloat16),
            pltpu.VMEM((seqs, tokens, 2 * rank), jnp.float32),
            pltpu.VMEM((seqs, max(t_size - 1, 1), tokens, 2 * rank), jnp.float32),
            pltpu.VMEM((rank, rank), jnp.float32),
            pltpu.VMEM((half, 3 * rank), jnp.bfloat16),
            pltpu.VMEM((3 * rank, rank), jnp.bfloat16),
            pltpu.VMEM((seqs, dp_size, rows, LANES), jnp.float32),
            pltpu.VMEM((dp_size, 8 * ((seqs + 7) // 8), LANES), jnp.int32),
            pltpu.VMEM((slots, rows, LANES), jnp.float32),
            pltpu.VMEM((8 * ((slots + 7) // 8), LANES), jnp.float32),
            pltpu.SMEM((seqs,), jnp.int32),
            pltpu.SMEM((seqs,), jnp.int32),
            pltpu.SMEM(owner.shape, jnp.int32),
            pltpu.VMEM((1, owner.shape[0]), jnp.int32),
            pltpu.VMEM((rank, rank), jnp.float32),
            pltpu.VMEM((rank, rank), jnp.float32),
            dma((seqs, pieces_of(hid_width))),
            dma((seqs,)),
            dma((2,)),
            dma((6,)),
            dma((seqs,)),
            dma((seqs,)),
            dma((seqs,)),
            dma((seqs,)),
            dma((seqs,)),
            dma((seqs,)),
            dma((1,)),
            dma((1,)),
            dma((1,)),
            dma((1,)),
        ],
        compiler_params=pltpu.CompilerParams(
            collective_id=0, has_side_effects=True, vmem_limit_bytes=64 * 1024 * 1024
        ),
        cost_estimate=pl.CostEstimate(
            flops=flops,
            bytes_accessed=2 * (seqs * tokens + rank) * (hid_width + og_width),
            transcendentals=0,
        ),
    )(
        lengths,
        language,
        owner,
        owner.reshape(1, -1),
        left_inv,
        right_inv,
        hidden,
        out_grad,
        proj_in,
        proj_out,
    )
    return pl.pallas_call(
        functools.partial(finish, slots),
        out_shape=(
            jax.ShapeDtypeStruct((seqs, half * rank), jnp.float32),
            jax.ShapeDtypeStruct((slots, half * rank), jnp.float32),
        ),
        in_specs=[vmem],
        out_specs=(vmem, vmem),
    )(blocks)


def solution(mesh):
    return jax.shard_map(
        per_device,
        mesh=mesh,
        in_specs=(
            P("dp", None, "tensor"),
            P("dp", None, "tensor"),
            P(None, "tensor"),
            P(None, "tensor"),
            P(),
            P(),
            P("dp"),
            P("dp"),
            P(),
        ),
        out_specs=(P("dp", "tensor"), P("dp", "tensor")),
        check_vma=False,
    )
```

```python
import functools
import math

import jax
import jax.numpy as jnp
from jax import lax
from jax.experimental import pallas as pl
from jax.experimental.pallas import tpu as pltpu
from jax.sharding import PartitionSpec as P

LANES = 128


def pieces_of(width):
    for count in (4, 2):
        if width % (count * 256) == 0:
            return count
    return 1


def halves(values):
    high = values.astype(jnp.bfloat16)
    return high, (values - high.astype(jnp.float32)).astype(jnp.bfloat16)


def finish(slots, rows_in, grads_out, means_out):
    rows = rows_in.shape[1]
    for n in range(rows_in.shape[0]):
        block = rows_in[n]
        for r in range(rows):
            cols = slice(r * LANES, (r + 1) * LANES)
            if n < slots:
                means_out[n : n + 1, cols] = block[r : r + 1]
            else:
                grads_out[n - slots : n - slots + 1, cols] = block[r : r + 1]


def kernel(
    sizes,
    lengths_in,
    language_in,
    owner_in,
    owner_row_in,
    left_inv_in,
    right_inv_in,
    hidden,
    out_grad,
    proj_in,
    proj_out,
    out,
    hid,
    og,
    w_in,
    w_out,
    part,
    peer_part,
    g_scr,
    l_split,
    r_split,
    gathered,
    places,
    sums,
    counts,
    lengths,
    language,
    owner_list,
    owner_row,
    left_inv,
    right_inv,
    hid_sem,
    og_sem,
    w_sem,
    small_sem,
    t_send,
    t_recv,
    z_send,
    z_recv,
    p_send,
    p_recv,
    d_send,
    d_recv,
    m_send,
    m_recv,
):
    t_size, outer, inner, slots = sizes
    seqs, tokens, hid_width = hid.shape
    rank = w_in.shape[0]
    half = rank // t_size
    rows = half // 2
    wide = 2 * rank
    dp = lax.axis_index("dp")
    t_me = lax.axis_index("tensor")
    my_out = dp // inner
    my_in = dp % inner
    me = my_in * outer + my_out
    last = seqs - 1
    hid_pieces = pieces_of(hid_width)
    piece = hid_width // hid_pieces
    cut = 256 * ((piece // 256 + 1) // 2)

    def og_copy(s):
        return pltpu.make_async_copy(out_grad.at[s], og.at[s], og_sem.at[s])

    def hid_copy(s, c):
        cols = pl.ds(pl.multiple_of(c * piece, LANES), piece)
        return pltpu.make_async_copy(
            hidden.at[s, :, cols], hid.at[s, :, cols], hid_sem.at[s, c]
        )

    w_in_copy = pltpu.make_async_copy(proj_in, w_in, w_sem.at[0])
    w_out_copy = pltpu.make_async_copy(proj_out, w_out, w_sem.at[1])
    small_copies = [
        pltpu.make_async_copy(source, target, small_sem.at[n])
        for n, (source, target) in enumerate(
            (
                (language_in, language),
                (owner_in, owner_list),
                (owner_row_in, owner_row),
                (lengths_in, lengths),
                (left_inv_in, left_inv),
                (right_inv_in, right_inv),
            )
        )
    ]
    w_out_copy.start()
    og_copy(0).start()
    w_in_copy.start()
    for copy in small_copies:
        copy.start()

    def start_piece(c, carry):
        hid_copy(0, c).start()
        return carry

    lax.fori_loop(0, hid_pieces, start_piece, None)

    def t_peer(k):
        return (dp, (t_me + k) % t_size)

    def z_peer(k):
        return (((my_out + k) % outer) * inner + my_in, t_me)

    def p_peer(k):
        return (my_out * inner + (my_in + k) % inner, t_me)

    others = outer * inner - 1

    def each_other(act):
        def visit(n, carry):
            act(((dp + 1 + (n + others // 2) % others) % (others + 1), t_me))
            return carry

        if others:
            lax.fori_loop(0, others, visit, None)

    barrier = pltpu.get_barrier_semaphore()

    def greet(peer):
        pl.semaphore_signal(
            barrier, inc=1, device_id=peer, device_id_type=pl.DeviceIdType.MESH
        )

    for k in range(1, t_size):
        greet(t_peer(k))
    each_other(greet)

    for copy in small_copies:
        copy.wait()
    own_row = owner_row[...]
    lang_lane = lax.broadcasted_iota(jnp.int32, own_row.shape, 1)
    sub = lax.broadcasted_iota(jnp.int32, places.shape[1:], 0)
    place_block = jnp.full(places.shape[1:], -1, jnp.int32)
    for s in range(seqs):
        lang = language[s]
        own = owner_list[lang]
        earlier = (own_row == own) & (lang_lane < lang)
        slot = jnp.sum(earlier.astype(jnp.int32), axis=1, keepdims=True)
        place_block = jnp.where(sub == s, own * slots + slot, place_block)
    places[me] = place_block
    sums[...] = jnp.zeros_like(sums)
    counts[...] = jnp.zeros_like(counts)

    def send(src, dst, send_sem, recv_sem, peer):
        pltpu.make_async_remote_copy(
            src_ref=src,
            dst_ref=dst,
            send_sem=send_sem,
            recv_sem=recv_sem,
            device_id=peer,
            device_id_type=pl.DeviceIdType.MESH,
        ).start()

    def take(block, sem):
        pltpu.make_async_copy(block, block, sem).wait()

    def project(s):
        dims = (((1,), (1,)), ((), ()))
        og_copy(s).wait()

        @pl.when(s + 1 < seqs)
        def _():
            og_copy(s + 1).start()

        right = lax.dot_general(w_out[...], og[s], dims, preferred_element_type=jnp.float32)
        part[s, rank:wide, :] = right

        def add_piece(c, left):
            hid_copy(s, c).wait()

            @pl.when(s + 1 < seqs)
            def _():
                hid_copy(s + 1, c).start()

            base = pl.multiple_of(c * piece, LANES)
            for begin, end in ((0, cut), (cut, piece)):
                cols = pl.ds(base + begin, end - begin)
                left += lax.dot_general(
                    w_in[:, cols], hid[s, :, cols], dims, preferred_element_type=jnp.float32
                )
            return left

        part[s, 0:rank, :] = lax.fori_loop(
            0, hid_pieces, add_piece, jnp.zeros((rank, tokens), jnp.float32)
        )
        for k in range(1, t_size):
            for q in range(4):
                some = pl.ds(q * (wide // 4), wide // 4)
                send(
                    part.at[s, some],
                    peer_part.at[s, k - 1, some],
                    t_send.at[s],
                    t_recv.at[s],
                    t_peer(k),
                )

    first = t_me * half
    even = pl.ds(first, rows, stride=2)
    odd = pl.ds(first + 1, rows, stride=2)

    def reduce(s):
        if t_size > 1:
            take(peer_part.at[s], t_recv.at[s])
        both = part[s]
        for k in range(1, t_size):
            both += peer_part[s, k - 1]
        token = lax.broadcasted_iota(jnp.int32, both.shape, 1)
        both = jnp.where(token < lengths[s], both, 0.0)
        high, low = halves(both)
        split = jnp.concatenate([high, low], axis=0)
        full = lax.dot_general(
            split, split, (((1,), (1,)), ((), ())), preferred_element_type=jnp.float32
        )
        full = full[0:rank] + full[wide : wide + rank]
        full = full[:, 0:wide] + full[:, wide : 2 * wide]
        grads = full[:, rank:wide]
        g_scr[...] = grads
        high, low = halves(grads)
        done = jnp.dot(
            l_split[...],
            jnp.concatenate([high, low, high], axis=0),
            preferred_element_type=jnp.float32,
        )
        high, low = halves(done)
        pre = jnp.dot(
            jnp.concatenate([high, low, high], axis=1),
            r_split[...],
            preferred_element_type=jnp.float32,
        )
        gathered[s, me] = jnp.concatenate([pre[:rows], pre[rows:]], axis=1)
        block = gathered.at[s, me]

        @pl.when(s < last)
        def _():
            for k in range(1, outer):
                send(block, block, z_send.at[s], z_recv.at[s], z_peer(k))

        @pl.when(s == last)
        def _():
            each_other(lambda peer: send(block, block, d_send.at[0], d_recv.at[0], peer))

        out[slots + s] = jnp.concatenate([g_scr[even, :], g_scr[odd, :]], axis=1)

    def forward(s):
        if outer > 1:
            take(gathered.at[s, pl.ds(0, outer - 1)], z_recv.at[s])
        block = gathered.at[s, pl.ds(my_in * outer, outer)]
        for k in range(1, inner):
            send(block, block, p_send.at[s], p_recv.at[s], p_peer(k))

    def accumulate(s):
        if others:

            @pl.when(s == 0)
            def _():
                take(places.at[pl.ds(0, others)], m_recv.at[0])

            @pl.when(s == last)
            def _():
                take(gathered.at[last, pl.ds(0, others)], d_recv.at[0])

        if inner > 1:

            @pl.when(s < last)
            def _():
                take(gathered.at[s, pl.ds(0, (inner - 1) * outer)], p_recv.at[s])

        def add_block(i, held):
            total, seen = list(held[0]), list(held[1])
            for o in range(outer):
                place = places[i * outer + o, pl.ds(s, 1), :]
                row = gathered[s, i * outer + o]
                for j in range(slots):
                    hit = (place == dp * slots + j).astype(jnp.float32)
                    total[j] = total[j] + hit * row
                    seen[j] = seen[j] + hit
            return tuple(total), tuple(seen)

        total, seen = lax.fori_loop(
            0,
            inner,
            add_block,
            (
                tuple(sums[j] for j in range(slots)),
                tuple(counts[pl.ds(j, 1), :] for j in range(slots)),
            ),
        )
        for j in range(slots):
            sums[j] = total[j]
            counts[pl.ds(j, 1), :] = seen[j]

    w_out_copy.wait()
    w_in_copy.wait()
    pl.semaphore_wait(barrier, t_size - 1 + others)
    own_places = places.at[me]
    each_other(lambda peer: send(own_places, own_places, m_send.at[0], m_recv.at[0], peer))

    left_rows = jnp.concatenate([left_inv[even, :], left_inv[odd, :]], axis=0)
    high, low = halves(left_rows)
    l_split[...] = jnp.concatenate([high, high, low], axis=1)
    high, low = halves(right_inv[...])
    r_split[...] = jnp.concatenate([high, high, low], axis=0)

    def step(i, carry):
        @pl.when(i < seqs)
        def _():
            project(i)

        @pl.when((i >= 1) & (i <= seqs))
        def _():
            reduce(i - 1)

        @pl.when((i >= 2) & (i <= seqs))
        def _():
            forward(i - 2)

        @pl.when(i >= 3)
        def _():
            accumulate(i - 3)

        return carry

    lax.fori_loop(0, seqs + 3, step, None)
    for j in range(slots):
        out[j] = sums[j] / jnp.maximum(counts[pl.ds(j, 1), :], 1.0)

    for s in range(seqs):
        if t_size > 1:
            take(peer_part.at[s], t_send.at[s])
    for s in range(last):
        if outer > 1:
            take(gathered.at[s, pl.ds(0, outer - 1)], z_send.at[s])
        if inner > 1:
            take(gathered.at[s, pl.ds(0, (inner - 1) * outer)], p_send.at[s])
    if others:
        take(gathered.at[last, pl.ds(0, others)], d_send.at[0])
        take(places.at[pl.ds(0, others)], m_send.at[0])


def per_device(hidden, out_grad, proj_in, proj_out, left_inv, right_inv, lengths, language, owner):
    seqs, tokens, hid_width = hidden.shape
    og_width = out_grad.shape[2]
    rank = proj_in.shape[0]
    t_size = lax.axis_size("tensor")
    dp_size = lax.axis_size("dp")
    inner = 2 ** (int(math.log2(dp_size)) // 2)
    while dp_size % inner:
        inner -= 1
    outer = dp_size // inner
    slots = (owner.shape[0] + dp_size - 1) // dp_size
    half = rank // t_size
    rows = half * rank // LANES
    vmem = pl.BlockSpec(memory_space=pltpu.VMEM)
    anywhere = pl.BlockSpec(memory_space=pl.ANY)
    dma = pltpu.SemaphoreType.DMA
    flops = 2 * seqs * tokens * rank * (hid_width + og_width)
    blocks = pl.pallas_call(
        functools.partial(kernel, (t_size, outer, inner, slots)),
        out_shape=jax.ShapeDtypeStruct((slots + seqs, rows, LANES), jnp.float32),
        in_specs=[anywhere] * 10,
        out_specs=vmem,
        scratch_shapes=[
            pltpu.VMEM((seqs, tokens, hid_width), jnp.bfloat16),
            pltpu.VMEM((seqs, tokens, og_width), jnp.bfloat16),
            pltpu.VMEM((rank, hid_width), jnp.bfloat16),
            pltpu.VMEM((rank, og_width), jnp.bfloat16),
            pltpu.VMEM((seqs, 2 * rank, tokens), jnp.float32),
            pltpu.VMEM((seqs, max(t_size - 1, 1), 2 * rank, tokens), jnp.float32),
            pltpu.VMEM((rank, rank), jnp.float32),
            pltpu.VMEM((half, 3 * rank), jnp.bfloat16),
            pltpu.VMEM((3 * rank, rank), jnp.bfloat16),
            pltpu.VMEM((seqs, dp_size, rows, LANES), jnp.float32),
            pltpu.VMEM((dp_size, 8 * ((seqs + 7) // 8), LANES), jnp.int32),
            pltpu.VMEM((slots, rows, LANES), jnp.float32),
            pltpu.VMEM((8 * ((slots + 7) // 8), LANES), jnp.float32),
            pltpu.SMEM((seqs,), jnp.int32),
            pltpu.SMEM((seqs,), jnp.int32),
            pltpu.SMEM(owner.shape, jnp.int32),
            pltpu.VMEM((1, owner.shape[0]), jnp.int32),
            pltpu.VMEM((rank, rank), jnp.float32),
            pltpu.VMEM((rank, rank), jnp.float32),
            dma((seqs, pieces_of(hid_width))),
            dma((seqs,)),
            dma((2,)),
            dma((6,)),
            dma((seqs,)),
            dma((seqs,)),
            dma((seqs,)),
            dma((seqs,)),
            dma((seqs,)),
            dma((seqs,)),
            dma((1,)),
            dma((1,)),
            dma((1,)),
            dma((1,)),
        ],
        compiler_params=pltpu.CompilerParams(
            collective_id=0, has_side_effects=True, vmem_limit_bytes=64 * 1024 * 1024
        ),
        cost_estimate=pl.CostEstimate(
            flops=flops,
            bytes_accessed=2 * (seqs * tokens + rank) * (hid_width + og_width),
            transcendentals=0,
        ),
    )(
        lengths,
        language,
        owner,
        owner.reshape(1, -1),
        left_inv,
        right_inv,
        hidden,
        out_grad,
        proj_in,
        proj_out,
    )
    return pl.pallas_call(
        functools.partial(finish, slots),
        out_shape=(
            jax.ShapeDtypeStruct((seqs, half * rank), jnp.float32),
            jax.ShapeDtypeStruct((slots, half * rank), jnp.float32),
        ),
        in_specs=[vmem],
        out_specs=(vmem, vmem),
    )(blocks)


def solution(mesh):
    return jax.shard_map(
        per_device,
        mesh=mesh,
        in_specs=(
            P("dp", None, "tensor"),
            P("dp", None, "tensor"),
            P(None, "tensor"),
            P(None, "tensor"),
            P(),
            P(),
            P("dp"),
            P("dp"),
            P(),
        ),
        out_specs=(P("dp", "tensor"), P("dp", "tensor")),
        check_vma=False,
    )
```

```python
import functools
import math

import jax
import jax.numpy as jnp
from jax import lax
from jax.experimental import pallas as pl
from jax.experimental.pallas import tpu as pltpu
from jax.sharding import PartitionSpec as P

LANES = 128


def pieces_of(width):
    for count in (4, 2):
        if width % (count * 256) == 0:
            return count
    return 1


def halves(values):
    high = values.astype(jnp.bfloat16)
    return high, (values - high.astype(jnp.float32)).astype(jnp.bfloat16)


def finish(slots, rows_in, grads_out, means_out):
    rows = rows_in.shape[1]
    for n in range(rows_in.shape[0]):
        block = rows_in[n]
        for r in range(rows):
            cols = slice(r * LANES, (r + 1) * LANES)
            if n < slots:
                means_out[n : n + 1, cols] = block[r : r + 1]
            else:
                grads_out[n - slots : n - slots + 1, cols] = block[r : r + 1]


def kernel(
    sizes,
    lengths_in,
    language_in,
    owner_in,
    owner_row_in,
    left_inv_in,
    right_inv_in,
    hidden,
    out_grad,
    proj_in,
    proj_out,
    out,
    hid,
    og,
    w_in,
    w_out,
    part,
    peer_part,
    g_scr,
    l_split,
    r_split,
    gathered,
    places,
    sums,
    counts,
    lengths,
    language,
    owner_list,
    owner_row,
    left_inv,
    right_inv,
    hid_sem,
    og_sem,
    w_sem,
    small_sem,
    t_send,
    t_recv,
    z_send,
    z_recv,
    p_send,
    p_recv,
    d_send,
    d_recv,
    m_send,
    m_recv,
):
    t_size, outer, inner, slots = sizes
    seqs, tokens, hid_width = hid.shape
    rank = w_in.shape[0]
    half = rank // t_size
    rows = half // 2
    wide = 2 * rank
    dp = lax.axis_index("dp")
    t_me = lax.axis_index("tensor")
    my_out = dp // inner
    my_in = dp % inner
    me = my_in * outer + my_out
    last = seqs - 1
    hid_pieces = pieces_of(hid_width)
    piece = hid_width // hid_pieces
    cut = 256 * ((piece // 256 + 1) // 2)

    def og_copy(s):
        return pltpu.make_async_copy(out_grad.at[s], og.at[s], og_sem.at[s])

    def hid_copy(s, c):
        cols = pl.ds(pl.multiple_of(c * piece, LANES), piece)
        return pltpu.make_async_copy(
            hidden.at[s, :, cols], hid.at[s, :, cols], hid_sem.at[s, c]
        )

    w_in_copy = pltpu.make_async_copy(proj_in, w_in, w_sem.at[0])
    w_out_copy = pltpu.make_async_copy(proj_out, w_out, w_sem.at[1])
    small_copies = [
        pltpu.make_async_copy(source, target, small_sem.at[n])
        for n, (source, target) in enumerate(
            (
                (language_in, language),
                (owner_in, owner_list),
                (owner_row_in, owner_row),
                (lengths_in, lengths),
                (left_inv_in, left_inv),
                (right_inv_in, right_inv),
            )
        )
    ]
    w_out_copy.start()
    og_copy(0).start()
    w_in_copy.start()
    for copy in small_copies:
        copy.start()

    def start_piece(c, carry):
        hid_copy(0, c).start()
        return carry

    lax.fori_loop(0, hid_pieces, start_piece, None)

    def t_peer(k):
        return (dp, (t_me + k) % t_size)

    def z_peer(k):
        return (((my_out + k) % outer) * inner + my_in, t_me)

    def p_peer(k):
        return (my_out * inner + (my_in + k) % inner, t_me)

    others = outer * inner - 1

    def each_other(act):
        def visit(n, carry):
            act(((dp + 1 + (n + others // 2) % others) % (others + 1), t_me))
            return carry

        if others:
            lax.fori_loop(0, others, visit, None)

    barrier = pltpu.get_barrier_semaphore()

    def greet(peer):
        pl.semaphore_signal(
            barrier, inc=1, device_id=peer, device_id_type=pl.DeviceIdType.MESH
        )

    for k in range(1, t_size):
        greet(t_peer(k))
    each_other(greet)

    for copy in small_copies:
        copy.wait()
    own_row = owner_row[...]
    lang_lane = lax.broadcasted_iota(jnp.int32, own_row.shape, 1)
    sub = lax.broadcasted_iota(jnp.int32, places.shape[1:], 0)
    place_block = jnp.full(places.shape[1:], -1, jnp.int32)
    for s in range(seqs):
        lang = language[s]
        own = owner_list[lang]
        earlier = (own_row == own) & (lang_lane < lang)
        slot = jnp.sum(earlier.astype(jnp.int32), axis=1, keepdims=True)
        place_block = jnp.where(sub == s, own * slots + slot, place_block)
    places[me] = place_block
    sums[...] = jnp.zeros_like(sums)
    counts[...] = jnp.zeros_like(counts)

    def send(src, dst, send_sem, recv_sem, peer):
        pltpu.make_async_remote_copy(
            src_ref=src,
            dst_ref=dst,
            send_sem=send_sem,
            recv_sem=recv_sem,
            device_id=peer,
            device_id_type=pl.DeviceIdType.MESH,
        ).start()

    def take(block, sem):
        pltpu.make_async_copy(block, block, sem).wait()

    def project(s):
        dims = (((1,), (1,)), ((), ()))
        og_copy(s).wait()

        @pl.when(s + 1 < seqs)
        def _():
            og_copy(s + 1).start()

        right = lax.dot_general(w_out[...], og[s], dims, preferred_element_type=jnp.float32)
        part[s, rank:wide, :] = right

        def add_piece(c, left):
            @pl.when((c == hid_pieces // 2) & (s >= 2))
            def _():
                reduce(s - 2)

            hid_copy(s, c).wait()

            @pl.when(s + 1 < seqs)
            def _():
                hid_copy(s + 1, c).start()

            base = pl.multiple_of(c * piece, LANES)
            for begin, end in ((0, cut), (cut, piece)):
                cols = pl.ds(base + begin, end - begin)
                left += lax.dot_general(
                    w_in[:, cols], hid[s, :, cols], dims, preferred_element_type=jnp.float32
                )
            return left

        part[s, 0:rank, :] = lax.fori_loop(
            0, hid_pieces, add_piece, jnp.zeros((rank, tokens), jnp.float32)
        )
        for k in range(1, t_size):
            for q in range(4):
                some = pl.ds(q * (wide // 4), wide // 4)
                send(
                    part.at[s, some],
                    peer_part.at[s, k - 1, some],
                    t_send.at[s],
                    t_recv.at[s],
                    t_peer(k),
                )

    first = t_me * half
    even = pl.ds(first, rows, stride=2)
    odd = pl.ds(first + 1, rows, stride=2)

    def reduce(s):
        if t_size > 1:
            take(peer_part.at[s], t_recv.at[s])
        both = part[s]
        for k in range(1, t_size):
            both += peer_part[s, k - 1]
        token = lax.broadcasted_iota(jnp.int32, both.shape, 1)
        both = jnp.where(token < lengths[s], both, 0.0)
        high, low = halves(both)
        split = jnp.concatenate([high, low], axis=0)
        full = lax.dot_general(
            split, split, (((1,), (1,)), ((), ())), preferred_element_type=jnp.float32
        )
        full = full[0:rank] + full[wide : wide + rank]
        full = full[:, 0:wide] + full[:, wide : 2 * wide]
        grads = full[:, rank:wide]
        g_scr[...] = grads
        high, low = halves(grads)
        done = jnp.dot(
            l_split[...],
            jnp.concatenate([high, low, high], axis=0),
            preferred_element_type=jnp.float32,
        )
        high, low = halves(done)
        pre = jnp.dot(
            jnp.concatenate([high, low, high], axis=1),
            r_split[...],
            preferred_element_type=jnp.float32,
        )
        gathered[s, me] = jnp.concatenate([pre[:rows], pre[rows:]], axis=1)
        block = gathered.at[s, me]

        @pl.when(s < last)
        def _():
            for k in range(1, outer):
                send(block, block, z_send.at[s], z_recv.at[s], z_peer(k))

        @pl.when(s == last)
        def _():
            each_other(lambda peer: send(block, block, d_send.at[0], d_recv.at[0], peer))

        out[slots + s] = jnp.concatenate([g_scr[even, :], g_scr[odd, :]], axis=1)

    def forward(s):
        if outer > 1:
            take(gathered.at[s, pl.ds(0, outer - 1)], z_recv.at[s])
        block = gathered.at[s, pl.ds(my_in * outer, outer)]
        for k in range(1, inner):
            send(block, block, p_send.at[s], p_recv.at[s], p_peer(k))

    def accumulate(s):
        if others:

            @pl.when(s == 0)
            def _():
                take(places.at[pl.ds(0, others)], m_recv.at[0])

            @pl.when(s == last)
            def _():
                take(gathered.at[last, pl.ds(0, others)], d_recv.at[0])

        if inner > 1:

            @pl.when(s < last)
            def _():
                take(gathered.at[s, pl.ds(0, (inner - 1) * outer)], p_recv.at[s])

        def add_block(i, held):
            total, seen = list(held[0]), list(held[1])
            for o in range(outer):
                place = places[i * outer + o, pl.ds(s, 1), :]
                row = gathered[s, i * outer + o]
                for j in range(slots):
                    hit = (place == dp * slots + j).astype(jnp.float32)
                    total[j] = total[j] + hit * row
                    seen[j] = seen[j] + hit
            return tuple(total), tuple(seen)

        total, seen = lax.fori_loop(
            0,
            inner,
            add_block,
            (
                tuple(sums[j] for j in range(slots)),
                tuple(counts[pl.ds(j, 1), :] for j in range(slots)),
            ),
        )
        for j in range(slots):
            sums[j] = total[j]
            counts[pl.ds(j, 1), :] = seen[j]

    w_out_copy.wait()
    w_in_copy.wait()
    pl.semaphore_wait(barrier, t_size - 1 + others)
    own_places = places.at[me]
    each_other(lambda peer: send(own_places, own_places, m_send.at[0], m_recv.at[0], peer))

    left_rows = jnp.concatenate([left_inv[even, :], left_inv[odd, :]], axis=0)
    high, low = halves(left_rows)
    l_split[...] = jnp.concatenate([high, high, low], axis=1)
    high, low = halves(right_inv[...])
    r_split[...] = jnp.concatenate([high, high, low], axis=0)

    def project_step(s, carry):
        project(s)
        return carry

    def reduce_step(s, carry):
        reduce(s)

        @pl.when(s >= 1)
        def _():
            forward(s - 1)

        return carry

    def accumulate_step(s, carry):
        accumulate(s)
        return carry

    lax.fori_loop(0, seqs, project_step, None)
    for s in range(seqs - 3):
        forward(s)
    lax.fori_loop(max(seqs - 2, 0), seqs, reduce_step, None)
    lax.fori_loop(0, seqs, accumulate_step, None)
    for j in range(slots):
        out[j] = sums[j] / jnp.maximum(counts[pl.ds(j, 1), :], 1.0)

    for s in range(seqs):
        if t_size > 1:
            take(peer_part.at[s], t_send.at[s])
    for s in range(last):
        if outer > 1:
            take(gathered.at[s, pl.ds(0, outer - 1)], z_send.at[s])
        if inner > 1:
            take(gathered.at[s, pl.ds(0, (inner - 1) * outer)], p_send.at[s])
    if others:
        take(gathered.at[last, pl.ds(0, others)], d_send.at[0])
        take(places.at[pl.ds(0, others)], m_send.at[0])


def per_device(hidden, out_grad, proj_in, proj_out, left_inv, right_inv, lengths, language, owner):
    seqs, tokens, hid_width = hidden.shape
    og_width = out_grad.shape[2]
    rank = proj_in.shape[0]
    t_size = lax.axis_size("tensor")
    dp_size = lax.axis_size("dp")
    inner = 2 ** (int(math.log2(dp_size)) // 2)
    while dp_size % inner:
        inner -= 1
    outer = dp_size // inner
    slots = (owner.shape[0] + dp_size - 1) // dp_size
    half = rank // t_size
    rows = half * rank // LANES
    vmem = pl.BlockSpec(memory_space=pltpu.VMEM)
    anywhere = pl.BlockSpec(memory_space=pl.ANY)
    dma = pltpu.SemaphoreType.DMA
    flops = 2 * seqs * tokens * rank * (hid_width + og_width)
    blocks = pl.pallas_call(
        functools.partial(kernel, (t_size, outer, inner, slots)),
        out_shape=jax.ShapeDtypeStruct((slots + seqs, rows, LANES), jnp.float32),
        in_specs=[anywhere] * 10,
        out_specs=vmem,
        scratch_shapes=[
            pltpu.VMEM((seqs, tokens, hid_width), jnp.bfloat16),
            pltpu.VMEM((seqs, tokens, og_width), jnp.bfloat16),
            pltpu.VMEM((rank, hid_width), jnp.bfloat16),
            pltpu.VMEM((rank, og_width), jnp.bfloat16),
            pltpu.VMEM((seqs, 2 * rank, tokens), jnp.float32),
            pltpu.VMEM((seqs, max(t_size - 1, 1), 2 * rank, tokens), jnp.float32),
            pltpu.VMEM((rank, rank), jnp.float32),
            pltpu.VMEM((half, 3 * rank), jnp.bfloat16),
            pltpu.VMEM((3 * rank, rank), jnp.bfloat16),
            pltpu.VMEM((seqs, dp_size, rows, LANES), jnp.float32),
            pltpu.VMEM((dp_size, 8 * ((seqs + 7) // 8), LANES), jnp.int32),
            pltpu.VMEM((slots, rows, LANES), jnp.float32),
            pltpu.VMEM((8 * ((slots + 7) // 8), LANES), jnp.float32),
            pltpu.SMEM((seqs,), jnp.int32),
            pltpu.SMEM((seqs,), jnp.int32),
            pltpu.SMEM(owner.shape, jnp.int32),
            pltpu.VMEM((1, owner.shape[0]), jnp.int32),
            pltpu.VMEM((rank, rank), jnp.float32),
            pltpu.VMEM((rank, rank), jnp.float32),
            dma((seqs, pieces_of(hid_width))),
            dma((seqs,)),
            dma((2,)),
            dma((6,)),
            dma((seqs,)),
            dma((seqs,)),
            dma((seqs,)),
            dma((seqs,)),
            dma((seqs,)),
            dma((seqs,)),
            dma((1,)),
            dma((1,)),
            dma((1,)),
            dma((1,)),
        ],
        compiler_params=pltpu.CompilerParams(
            collective_id=0, has_side_effects=True, vmem_limit_bytes=64 * 1024 * 1024
        ),
        cost_estimate=pl.CostEstimate(
            flops=flops,
            bytes_accessed=2 * (seqs * tokens + rank) * (hid_width + og_width),
            transcendentals=0,
        ),
    )(
        lengths,
        language,
        owner,
        owner.reshape(1, -1),
        left_inv,
        right_inv,
        hidden,
        out_grad,
        proj_in,
        proj_out,
    )
    return pl.pallas_call(
        functools.partial(finish, slots),
        out_shape=(
            jax.ShapeDtypeStruct((seqs, half * rank), jnp.float32),
            jax.ShapeDtypeStruct((slots, half * rank), jnp.float32),
        ),
        in_specs=[vmem],
        out_specs=(vmem, vmem),
    )(blocks)


def solution(mesh):
    return jax.shard_map(
        per_device,
        mesh=mesh,
        in_specs=(
            P("dp", None, "tensor"),
            P("dp", None, "tensor"),
            P(None, "tensor"),
            P(None, "tensor"),
            P(),
            P(),
            P("dp"),
            P("dp"),
            P(),
        ),
        out_specs=(P("dp", "tensor"), P("dp", "tensor")),
        check_vma=False,
    )
```
